128 devices in a mesh: exp: 32 (over x, y, core), tp: 4 (over z).
Axes of the slice: x: 4, y: 4, z: 4, core: 2. Of those that a mesh axis runs over, the one named last changes fastest.
Arguments:
- audio_feats: bfloat16 [16384, 1280], P(('exp', 'tp')), may hold values from -6 to 6
- w_audio: bfloat16 [1280, 2048], P(None, 'tp'), may hold values from -0.15625 to 0.15625
- b_audio: float32 [2048], replicated, may hold values from -3 to 3
- segments: int32 [32, 512], P('exp'), may hold values from 0 to 3, never falling along the last dimension, each value on 1 to 256 neighbouring positions
- w_q: bfloat16 [2048, 4096], P(None, 'tp'), may hold values from -0.125 to 0.125
- w_k: bfloat16 [2048, 512], P(None, 'tp'), may hold values from -0.125 to 0.125
- w_v: bfloat16 [2048, 512], P(None, 'tp'), may hold values from -0.125 to 0.125
- w_o: bfloat16 [4096, 2048], P('tp'), may hold values from -0.09375 to 0.09375
- attn_gain: float32 [2048], replicated, may hold values from 0.1 to 1.9
- q_gain: float32 [128], replicated, may hold values from 0.5 to 2
- k_gain: float32 [128], replicated, may hold values from 0.5 to 2
- moe_gain: float32 [2048], replicated, may hold values from 0.1 to 1.9
- w_router: bfloat16 [2048, 128], replicated
- routes: int32 [16384, 8], P(('exp', 'tp')), may hold values from 0 to 127, all different within a row; in each aligned block of 128 rows (0 to 127, 128 to 255, ...) at most 16 rows name the same one
- w_gate_up: bfloat16 [128, 2048, 1536], P(('exp', 'tp')), may hold values from -0.125 to 0.125
- w_down: bfloat16 [128, 768, 2048], P(('exp', 'tp')), may hold values from -0.625 to 0.625
Outputs:
- mixed: bfloat16 [16384, 2048], P(('exp', 'tp'))
The draws below stay inside these ranges and needn't reach their ends.
Inputs may be any that keep to these rules, and one draw needn't show every extreme that they name: `routes`: among the tokens of one device (aligned blocks of 128 rows) no expert id is named more than 16 times, a bound that some block reaches; the ids of one token differ. `segments`: ids never fall along a sequence; each id holds 1 to 256 positions, some exactly that many.
All inputs are finite; a program needn't handle non-finite values.
Results may differ from the reference program's by a relative error of at most 0.02.
Values may be sent and summed in bfloat16 or wider, within the bound.
No kernel may reach another device: no remote copies, remote signals or barrier semaphores. Data moves between devices by JAX's collectives and lax.ppermute only.
A program may use at most 128 MiB of HBM per device.

```python
import math
import jax
import jax.numpy as jnp
import numpy as np
from jax import lax

D = 2048
AUDIO = 1280
HEADS = 32
KV = 4
HD = 128
FF = 768
TOP = 8
ROWS = 128
DOCS = 4
EXPERTS = 128
SEQ = 512
TOKENS = 16384
CAP = 16
N_EXP = 32
N_TP = 4


def draw_w_router(key, part):
    key = jax.random.fold_in(key, 11)
    spread = 0.35 / jnp.sqrt(jnp.float32(D))
    values = jnp.clip(jax.random.normal(key, (D, EXPERTS), jnp.float32), -3.0, 3.0) * spread
    return values.astype(jnp.bfloat16)


def draw_q_gain(key, part):
    key = jax.random.fold_in(key, 12)
    return jnp.exp(jax.random.uniform(key, (HD,), jnp.float32, jnp.log(0.7), jnp.log(1.8)))


def draw_k_gain(key, part):
    key = jax.random.fold_in(key, 13)
    return jnp.exp(jax.random.uniform(key, (HD,), jnp.float32, jnp.log(0.7), jnp.log(1.8)))


def levels(stream_key, dims, split, low, largest):
    loudness = 1.0
    for position, shards_of in split:
        steps = jax.random.uniform(jax.random.fold_in(jax.random.fold_in(stream_key, 6), position), (shards_of,), jnp.float32, low / len(split), largest / len(split))
        loudness = loudness * jnp.repeat(jnp.exp(steps), dims[position] // shards_of).reshape((-1,) + (1,) * (len(dims) - 1 - position))
    return loudness


def length_profile(amount, total, limit, slope):
    portions = [(1 << 20) // math.isqrt(grade ** slope) + 1 for grade in range(2, amount + 1)]
    surplus, counts = total - limit - (amount - 1), [1] * (amount - 1)
    while surplus > 0:
        movable = [i for i in range(amount - 1) if counts[i] < limit]
        whole, remaining = sum([portions[i] for i in movable]), surplus
        for i in movable:
            extra = min(limit - counts[i], max(1, remaining * portions[i] // whole), surplus)
            counts[i] = counts[i] + extra
            surplus = surplus - extra
    return np.array([limit] + counts)


def uneven(rng, amount, total, bound, slope):
    if amount == 2:
        one = jax.random.randint(rng, (), max(1, total - bound), min(bound, total - 1) + 1)
        return jnp.stack([one, total - one])
    sizes = jnp.asarray(length_profile(amount, total, bound, slope), jnp.int32)
    twos = (amount - 1) // 2
    giver, taker = sizes[1:1 + 2 * twos:2], sizes[2:2 + 2 * twos:2]
    slack = jnp.minimum(giver - 1, bound - taker)
    passed = jax.random.randint(jax.random.fold_in(rng, 1), (twos,), 0, 1 << 20) % (slack + 1)
    sizes = sizes.at[1:1 + 2 * twos:2].set(giver - passed).at[2:2 + 2 * twos:2].set(taker + passed)
    return sizes[jax.random.permutation(jax.random.fold_in(rng, 2), amount)]


def deal_out(own_key, own, number, rows, number_of, top, reach, lean):
    sequence = jax.random.permutation(own_key, number_of)
    heavy_load, common = load_shares(number_of, rows * top, reach, lean, True), load_shares(number_of, rows * top, reach, lean, False)
    places = jnp.arange(number_of)

    def named(lengths, rotation):
        used = int((lengths > 0).sum())
        fixed = max(1, used // 4)
        passed = fixed + (places - fixed + rotation * (used - fixed)) % max(1, number_of - fixed)
        return jnp.zeros((number_of,), jnp.int32).at[sequence[jnp.where(places < fixed, places, passed)]].set(jnp.asarray(lengths, jnp.int32))

    lengths = jnp.where(number % 4 == 0, named(heavy_load, number // 4), named(common, number - number // 4 - 1))
    mixed = jax.random.permutation(jax.random.fold_in(own, 3), number_of)
    giver, sink = mixed[0:number_of // 2 * 2:2], mixed[1:number_of // 2 * 2:2]
    slack = jnp.minimum(lengths[giver] - 1, reach - lengths[sink]) // 2
    slack = jnp.where((giver == sequence[0]) | (sink == sequence[0]) | (lengths[sink] == 0), 0, jnp.maximum(slack, 0))
    passed = jax.random.randint(jax.random.fold_in(own, 4), (number_of // 2,), 0, 1 << 20) % (slack + 1)
    lengths = lengths.at[giver].add(-passed).at[sink].add(passed)
    labels = jnp.searchsorted(jnp.cumsum(lengths), jnp.arange(rows * top), side="right").astype(jnp.int32)
    table = labels.reshape(top, rows).T
    table = table[jax.random.permutation(jax.random.fold_in(own, 1), rows)]
    rotation = jax.random.randint(jax.random.fold_in(own, 2), (rows, 1), 0, top)
    return jnp.take_along_axis(table, (jnp.arange(top)[None, :] + rotation) % top, axis=1)


def load_shares(count, total, limit, skew, full):
    loads = [(1 << 20) // math.isqrt(grade ** skew) + 1 for grade in range(1, count + 1)]
    largest = limit if full else min(limit, max(-(-total // count), total * loads[0] // sum(loads)))
    least = 1 if total - largest >= count - 1 else 0
    counts, surplus = [largest] + [least] * (count - 1), total - largest - least * (count - 1)
    while surplus > 0:
        movable = [i for i in range(1, count) if counts[i] < largest] or [i for i in range(1, count) if counts[i] < limit]
        mass, budget = sum([loads[i] for i in movable]), surplus
        for i in movable:
            more = min(limit - counts[i], max(1, budget * loads[i] // mass), surplus)
            counts[i] = counts[i] + more
            surplus = surplus - more
    return np.array(counts)


def normal_values(own_key, extent, deviation, limit, shards=(), kind=jnp.bfloat16):
    array = jax.random.normal(own_key, extent, jnp.float32) * deviation
    if len(shards) > 0:
        array = levels(own_key, extent, shards, -0.22, 0.18) * array
    return jnp.clip(array, min=-limit, max=limit).astype(kind)


def setup_inputs(seed: int = 0) -> dict:
    arg_keys = jax.random.split(jax.random.key(seed), 17)
    audio_feats = normal_values(arg_keys[0], (TOKENS, AUDIO), 1.0, 6.0, ((0, 128),))
    w_audio = normal_values(arg_keys[1], (AUDIO, D), AUDIO ** -0.5, 0.15625, ((1, 4),))
    b_audio = normal_values(arg_keys[2], (D,), 0.5, 3.0, (), jnp.float32)
    segments = jax.vmap(lambda own: jnp.searchsorted(jnp.cumsum(uneven(own, DOCS, SEQ, SEQ // 2, 0)), jnp.arange(SEQ), side="right"))(jax.random.split(arg_keys[3], N_EXP)).reshape((N_EXP, SEQ)).astype(jnp.int32)
    w_q = normal_values(arg_keys[4], (D, HEADS * HD), D ** -0.5, 0.125, ((1, 4),))
    w_k = normal_values(arg_keys[5], (D, KV * HD), D ** -0.5, 0.125, ((1, 4),))
    w_v = normal_values(arg_keys[6], (D, KV * HD), D ** -0.5, 0.125, ((1, 4),))
    w_o = normal_values(arg_keys[7], (HEADS * HD, D), (HEADS * HD) ** -0.5, 0.09375, ((0, 4),))
    attn_gain = jnp.clip(1.0 + 0.18 * jax.random.normal(arg_keys[8], (D,), jnp.float32), 0.1, 1.9)
    q_gain = draw_q_gain(jax.random.fold_in(arg_keys[16], 71), 0)
    k_gain = draw_k_gain(jax.random.fold_in(arg_keys[16], 71), 0)
    moe_gain = jnp.clip(1.0 + 0.18 * jax.random.normal(arg_keys[11], (D,), jnp.float32), 0.1, 1.9)
    w_router = draw_w_router(jax.random.fold_in(arg_keys[16], 71), 0)
    routes_keys = jax.random.split(jax.random.fold_in(arg_keys[13], 1), TOKENS // ROWS)
    routes_turns = jax.random.permutation(jax.random.fold_in(arg_keys[13], 3), TOKENS // ROWS)
    routes = jax.vmap(lambda own, number: deal_out(jax.random.fold_in(arg_keys[13], 2), own, number, ROWS, EXPERTS, TOP, CAP, 2))(routes_keys, routes_turns).reshape((TOKENS, TOP))
    w_gate_up = normal_values(arg_keys[14], (EXPERTS, D, 2 * FF), D ** -0.5, 0.125, ((0, 128),))
    w_down = normal_values(arg_keys[15], (EXPERTS, FF, D), (FF // 9) ** -0.5, 0.625, ((0, 128),))
    return dict(audio_feats=audio_feats, w_audio=w_audio, b_audio=b_audio, segments=segments, w_q=w_q, w_k=w_k, w_v=w_v, w_o=w_o, attn_gain=attn_gain, q_gain=q_gain, k_gain=k_gain, moe_gain=moe_gain, w_router=w_router, routes=routes, w_gate_up=w_gate_up, w_down=w_down)


EPSILON = 1e-06
ROPE_BASE = 1000000.0

def rms_norm(values_in, gain_vec):
    squares = lax.optimization_barrier(jnp.mean(values_in * values_in, axis=-1, keepdims=True))
    return values_in * lax.rsqrt(squares + EPSILON) * gain_vec

def rope_tables(seq_len, head_dim):
    half_dim = head_dim // 2
    inv_freq = ROPE_BASE ** (-(jnp.arange(half_dim, dtype=jnp.float32) * 2.0) / head_dim)
    angles = jnp.arange(seq_len, dtype=jnp.float32)[:, None] * inv_freq[None, :]
    return (jnp.cos(angles)[:, None, :], jnp.sin(angles)[:, None, :])

def rotate(field, cos_table, sin_table):
    half_dim = field.shape[-1] // 2
    first = field[..., :half_dim]
    second = field[..., half_dim:]
    return jnp.concatenate([first * cos_table - second * sin_table, second * cos_table + first * sin_table], axis=-1)

def project_heads(normed, weight, gain_vec, head_count, cos_table, sin_table):
    raw = jnp.dot(normed, weight, preferred_element_type=jnp.float32)
    raw = raw.reshape(normed.shape[0], head_count, HD)
    return rotate(rms_norm(raw, gain_vec), cos_table, sin_table).astype(jnp.bfloat16)

def attend(x_seq, seg_ids, w_q, w_k, w_v, w_o, attn_gain, q_gain, k_gain):
    seq_len = x_seq.shape[0]
    cos_table, sin_table = rope_tables(seq_len, HD)
    normed = rms_norm(x_seq.astype(jnp.float32), attn_gain).astype(jnp.bfloat16)
    queries = project_heads(normed, w_q, q_gain, HEADS, cos_table, sin_table)
    keys_rot = project_heads(normed, w_k, k_gain, KV, cos_table, sin_table)
    values = jnp.dot(normed, w_v, preferred_element_type=jnp.float32).astype(jnp.bfloat16).reshape(seq_len, KV, HD)
    group = HEADS // KV
    grouped = queries.reshape(seq_len, KV, group, HD)
    scores = jnp.einsum('skgd,tkd->kgst', grouped.astype(jnp.float32), keys_rot.astype(jnp.float32)) / jnp.sqrt(jnp.float32(HD))
    index = jnp.arange(seq_len)
    allowed = (seg_ids[:, None] == seg_ids[None, :]) & (index[None, :] <= index[:, None])
    scores = jnp.where(allowed, scores, -jnp.inf)
    peak = lax.optimization_barrier(jnp.max(scores, axis=-1, keepdims=True))
    expo = jnp.exp(scores - peak)
    weights = (expo / lax.optimization_barrier(jnp.sum(expo, axis=-1, keepdims=True))).astype(jnp.bfloat16)
    context = jnp.einsum('kgst,tkd->skgd', weights.astype(jnp.float32), values.astype(jnp.float32))
    context = context.astype(jnp.bfloat16).reshape(seq_len, HEADS * HD)
    return jnp.dot(context, w_o, preferred_element_type=jnp.float32)

def reference(audio_feats, w_audio, b_audio, segments, w_q, w_k, w_v, w_o, attn_gain, q_gain, k_gain, moe_gain, w_router, routes, w_gate_up, w_down):
    tokens_x = (jnp.dot(audio_feats, w_audio, preferred_element_type=jnp.float32) + b_audio).astype(jnp.bfloat16)
    x_seqs = tokens_x.reshape(N_EXP, SEQ, D)

    def one_sequence(pair):
        return attend(pair[0], pair[1], w_q, w_k, w_v, w_o, attn_gain, q_gain, k_gain)
    attn_out = lax.map(one_sequence, (x_seqs, segments)).reshape(TOKENS, D)
    hidden_res = tokens_x.astype(jnp.float32) + attn_out
    normed = rms_norm(hidden_res, moe_gain).astype(jnp.bfloat16)
    logits = jnp.dot(normed, w_router, preferred_element_type=jnp.float32)
    chosen = jnp.take_along_axis(logits, routes, axis=1)
    gates = jax.nn.softmax(chosen, axis=-1).astype(jnp.bfloat16)
    flat_ids = routes.reshape(-1)
    flat_gates = gates.reshape(-1).astype(jnp.float32)
    most_rows = N_EXP * N_TP * CAP

    def one_expert(expert_id, running_sum):
        picked = flat_ids == expert_id
        index = jnp.nonzero(picked, size=most_rows, fill_value=0)[0].astype(jnp.int32)
        picked_count = jnp.sum(picked.astype(jnp.int32))
        valid = jnp.arange(most_rows, dtype=jnp.int32) < picked_count
        token_of = index // TOP
        rows_in = normed[token_of]
        gate_up = jnp.dot(rows_in, w_gate_up[expert_id], preferred_element_type=jnp.float32)
        hidden = (jax.nn.silu(gate_up[:, :FF]) * gate_up[:, FF:]).astype(jnp.bfloat16)
        expert_out = jnp.dot(hidden, w_down[expert_id], preferred_element_type=jnp.float32).astype(jnp.bfloat16)
        weight_of = jnp.where(valid, flat_gates[index], jnp.float32(0.0))
        return running_sum.at[token_of].add(weight_of[:, None] * expert_out.astype(jnp.float32))
    moe_out = lax.fori_loop(0, EXPERTS, one_expert, jnp.zeros((TOKENS, D), jnp.float32))
    return (hidden_res + moe_out).astype(jnp.bfloat16)
```

```python
import jax
import jax.numpy as jnp
from jax import lax
from jax.experimental import pallas as pl
from jax.experimental.pallas import tpu as pltpu
from jax.sharding import PartitionSpec as P

EPSILON = 1e-06
ROPE_BASE = 1000000.0
F32 = jnp.float32
BF16 = jnp.bfloat16
VMEM_BYTES = 48 * 1024 * 1024


def whole(count):
    return [pl.BlockSpec(memory_space=pltpu.VMEM)] * count


def shift(value, by):
    size = lax.axis_size("tp")
    return lax.ppermute(value, "tp", [(i, (i + by) % size) for i in range(size)])


def rope_tables(seq_len, head_dim):
    half_dim = head_dim // 2
    inv_freq = ROPE_BASE ** (-(jnp.arange(half_dim, dtype=F32) * 2.0) / head_dim)
    angles = jnp.arange(seq_len, dtype=F32)[:, None] * inv_freq[None, :]
    cos, sin = jnp.cos(angles), jnp.sin(angles)
    return jnp.concatenate([cos, cos], axis=1), jnp.concatenate([-sin, sin], axis=1)


def qkv_kernel(
    order, own, left, right, top, bottom, gain, w_q, w_k, w_v, q_gain, k_gain, cos, sin,
    q_out, k_out, v_out, normed,
):
    seq_len, width = own.shape
    half = seq_len // 2
    feat_dim = w_q.shape[0]
    head_dim = w_k.shape[1]
    for part in range(2):
        rows = pl.ds(part * half, half)
        pieces = [own[rows, :], left[rows, :], right[rows, :], (bottom if part else top)[...]]
        pieces = [piece.astype(F32) for piece in pieces]
        squares = sum(jnp.sum(piece * piece, axis=1, keepdims=True) for piece in pieces)
        scale = lax.rsqrt(squares / feat_dim + EPSILON)
        for place, piece in enumerate(pieces):
            at = order[place]
            columns = pl.ds(pl.multiple_of(at * width, width), width)
            normed[rows, columns] = (piece * scale * gain[pl.ds(at, 1), :]).astype(BF16)

    def head(raw, head_gain):
        squares = jnp.mean(raw * raw, axis=1, keepdims=True)
        raw = raw * lax.rsqrt(squares + EPSILON) * head_gain[...]
        return (raw * cos[...] + pltpu.roll(raw, head_dim // 2, 1) * sin[...]).astype(BF16)

    blocks, heads, rows_each, _ = q_out.shape
    for pair in range(heads // 2):
        raw = jnp.dot(
            normed[...], w_q[:, pl.ds(pair * 2 * head_dim, 2 * head_dim)],
            preferred_element_type=F32,
        )
        for one in range(2):
            rotated = head(raw[:, one * head_dim : (one + 1) * head_dim], q_gain)
            q_out[:, 2 * pair + one] = rotated.reshape(blocks, rows_each, head_dim)
    k_out[...] = head(jnp.dot(normed[...], w_k[...], preferred_element_type=F32), k_gain)
    v_out[...] = jnp.dot(normed[...], w_v[...], preferred_element_type=F32).astype(BF16)


def attend_kernel(which, queries, keys, values, seg_col, seg_row, w_o, out, context):
    blocks, heads, rows_each, head_dim = queries.shape
    block = which[0]

    for number in range(blocks):

        @pl.when(block == number)
        def _():
            span = (number + 1) * rows_each
            first = number * rows_each
            row_at = first + lax.broadcasted_iota(jnp.int32, (rows_each, span), 0)
            col_at = lax.broadcasted_iota(jnp.int32, (rows_each, span), 1)
            allowed = (seg_col[pl.ds(first, rows_each), :] == seg_row[:, :span]) & (col_at <= row_at)
            for head in range(heads):
                scores = lax.dot_general(
                    queries[number, head], keys[:span, :], (((1,), (1,)), ((), ())),
                    preferred_element_type=F32,
                ) * (float(head_dim) ** -0.5)
                scores = jnp.where(allowed, scores, -1e30)
                expo = jnp.exp(scores - jnp.max(scores, axis=1, keepdims=True))
                total = jnp.sum(expo, axis=1, keepdims=True)
                mixed = jnp.dot(expo.astype(BF16), values[:span, :], preferred_element_type=F32)
                context[:, pl.ds(head * head_dim, head_dim)] = (mixed / total).astype(BF16)

    out[...] = jnp.dot(context[...], w_o[...], preferred_element_type=F32).astype(BF16)


def expert_kernel(rows, w_gate_up, w_down, out):
    width = w_down.shape[0]
    both = jnp.dot(rows[...], w_gate_up[...], preferred_element_type=F32)
    gate, up = both[:, :width], both[:, width:]
    hidden = (gate * jax.nn.sigmoid(gate) * up).astype(BF16)
    out[...] = jnp.dot(hidden, w_down[...], preferred_element_type=F32).astype(BF16)


def run_expert(rows, w_gate_up, w_down):
    count, feat_dim = rows.shape
    width = w_down.shape[0]
    block = 256
    return pl.pallas_call(
        expert_kernel,
        grid=(count // block,),
        in_specs=[
            pl.BlockSpec((block, feat_dim), lambda i: (i, 0)),
            pl.BlockSpec((feat_dim, 2 * width), lambda i: (0, 0)),
            pl.BlockSpec((width, feat_dim), lambda i: (0, 0)),
        ],
        out_specs=pl.BlockSpec((block, feat_dim), lambda i: (i, 0)),
        out_shape=jax.ShapeDtypeStruct((count, feat_dim), BF16),
        compiler_params=pltpu.CompilerParams(vmem_limit_bytes=VMEM_BYTES),
        cost_estimate=pl.CostEstimate(
            flops=6 * count * feat_dim * width, transcendentals=count * width,
            bytes_accessed=4 * count * feat_dim + 6 * feat_dim * width,
        ),
        name="experts",
    )(rows, w_gate_up, w_down)


def on_device(
    audio_feats, w_audio, b_audio, segments, w_q, w_k, w_v, w_o, attn_gain, q_gain, k_gain,
    moe_gain, w_router, routes, w_gate_up, w_down,
):
    me = lax.axis_index("tp")
    tp_size = lax.axis_size("tp")
    tok_rows = audio_feats.shape[0]
    feat_dim = b_audio.shape[0]
    seq_len = segments.shape[1]
    head_dim = q_gain.shape[0]
    experts = w_router.shape[1]
    top_count = routes.shape[1]
    heads = w_q.shape[1] // head_dim
    width = w_audio.shape[1]
    slot_cap = max(4, 2 * tok_rows * top_count // experts)
    slots = experts * slot_cap

    seq_audio = jnp.zeros((tp_size,) + audio_feats.shape, BF16)
    for by in range(tp_size):
        piece = shift(audio_feats, by) if by else audio_feats
        at = lax.rem(me - by + tp_size, tp_size)
        seq_audio = lax.dynamic_update_slice_in_dim(seq_audio, piece[None], at, 0)
    seq_audio = seq_audio.reshape(seq_len, -1)

    expert_ids = jnp.arange(experts, dtype=jnp.int32)
    named = jnp.any(routes[:, :, None] == expert_ids[None, None, :], axis=1)
    earlier = (
        jnp.arange(tok_rows)[None, :] < jnp.arange(tok_rows)[:, None]
    ).astype(BF16)
    places = jnp.dot(earlier, named.astype(BF16), preferred_element_type=F32)
    places = jnp.where(named, places, -1.0).astype(BF16)
    slot_no = jnp.arange(slot_cap, dtype=jnp.int32).astype(BF16)
    dispatch = (places.T[:, None, :] == slot_no[None, :, None]).astype(BF16).reshape(slots, tok_rows)

    bias_part = lax.dynamic_slice_in_dim(b_audio, me * width, width, 0)
    columns = (jnp.dot(seq_audio, w_audio, preferred_element_type=F32) + bias_part).astype(BF16)
    half = seq_len // 2
    left = shift(columns, 1)
    right = shift(columns, -1)
    top = shift(left[:half], 1)
    bottom = shift(right[half:], -1)
    order = lax.rem(me + jnp.array([0, 3, 1, 2], jnp.int32), tp_size)

    cos, sin = rope_tables(seq_len, head_dim)
    queries, keys, values = pl.pallas_call(
        qkv_kernel,
        in_specs=[pl.BlockSpec(memory_space=pltpu.SMEM)] + whole(13),
        out_specs=whole(3),
        out_shape=(
            jax.ShapeDtypeStruct((tp_size, heads, tok_rows, head_dim), BF16),
            jax.ShapeDtypeStruct((seq_len, head_dim), BF16),
            jax.ShapeDtypeStruct((seq_len, head_dim), BF16),
        ),
        scratch_shapes=[pltpu.VMEM((seq_len, feat_dim), BF16)],
        compiler_params=pltpu.CompilerParams(vmem_limit_bytes=VMEM_BYTES),
        cost_estimate=pl.CostEstimate(
            flops=2 * seq_len * feat_dim * (heads + 2) * head_dim, transcendentals=seq_len * heads,
            bytes_accessed=2 * feat_dim * (seq_len + (heads + 2) * head_dim),
        ),
        name="project",
    )(
        order, columns, left, right, top, bottom, attn_gain.reshape(tp_size, width), w_q, w_k, w_v,
        q_gain[None], k_gain[None], cos, sin,
    )

    def attend(block):
        return pl.pallas_call(
            attend_kernel,
            in_specs=[pl.BlockSpec(memory_space=pltpu.SMEM)] + whole(6),
            out_specs=whole(1)[0],
            out_shape=jax.ShapeDtypeStruct((tok_rows, feat_dim), BF16),
            scratch_shapes=[pltpu.VMEM((tok_rows, heads * head_dim), BF16)],
            compiler_params=pltpu.CompilerParams(vmem_limit_bytes=VMEM_BYTES),
            cost_estimate=pl.CostEstimate(
                flops=2 * tok_rows * heads * head_dim * (2 * seq_len + feat_dim),
                transcendentals=tok_rows * heads * seq_len,
                bytes_accessed=2 * feat_dim * (heads * head_dim + tok_rows),
            ),
            name="attend",
        )(block[None], queries, keys, values, segments.reshape(seq_len, 1), segments, w_o)

    attn_out = None
    for by in (1, 3, 2, 0):
        piece = attend(lax.rem(me + by, tp_size))
        piece = (shift(piece, by) if by else piece).astype(F32)
        attn_out = piece if attn_out is None else attn_out + piece

    mine = me * tok_rows
    pieces = [
        lax.dynamic_slice_in_dim(piece, mine, tok_rows, 0) for piece in (columns, left, right)
    ]
    opposite = jnp.concatenate([top, bottom], axis=0)
    pieces.append(lax.dynamic_slice_in_dim(opposite, mine, tok_rows, 0))
    x_mine = jnp.zeros((tp_size, tok_rows, width), BF16)
    for place, piece in enumerate(pieces):
        x_mine = lax.dynamic_update_slice_in_dim(x_mine, piece[None], order[place], 0)
    x_mine = x_mine.transpose(1, 0, 2).reshape(tok_rows, feat_dim)

    hidden_res = x_mine.astype(F32) + attn_out
    squares = jnp.mean(hidden_res * hidden_res, axis=-1, keepdims=True)
    normed = (hidden_res * lax.rsqrt(squares + EPSILON) * moe_gain).astype(BF16)

    outgoing = jnp.dot(dispatch, normed, preferred_element_type=F32).astype(BF16)
    arrived = lax.all_to_all(
        outgoing.reshape(experts, slot_cap, feat_dim), ("exp", "tp"), 0, 0, tiled=True
    )

    expert_out = run_expert(arrived.reshape(slots, feat_dim), w_gate_up[0], w_down[0])
    returned = lax.all_to_all(
        expert_out.reshape(experts, slot_cap, feat_dim), ("exp", "tp"), 0, 0, tiled=True
    )

    logits = jnp.dot(normed, w_router, preferred_element_type=F32)
    peak = jnp.max(jnp.where(named, logits, -jnp.inf), axis=1, keepdims=True)
    expo = jnp.where(named, jnp.exp(jnp.minimum(logits - peak, 0.0)), 0.0)
    gates = (expo / jnp.sum(expo, axis=1, keepdims=True)).astype(BF16)
    slot_of = jnp.arange(slots, dtype=jnp.int32)
    spread = (expert_ids[:, None] == (slot_of // slot_cap)[None, :]).astype(BF16)
    wide_gates = jnp.dot(gates, spread, preferred_element_type=F32)
    wide_places = jnp.dot(places, spread, preferred_element_type=F32)
    combine = jnp.where(
        wide_places == (slot_of % slot_cap).astype(F32)[None, :], wide_gates, 0.0
    ).astype(BF16)
    moe_out = jnp.dot(combine, returned.reshape(slots, feat_dim), preferred_element_type=F32)
    return (hidden_res + moe_out).astype(BF16)


def solution(mesh):
    in_specs = (
        P(("exp", "tp"), None),
        P(None, "tp"),
        P(),
        P("exp", None),
        P(None, "tp"),
        P(None, "tp"),
        P(None, "tp"),
        P("tp", None),
        P(),
        P(),
        P(),
        P(),
        P(),
        P(("exp", "tp"), None),
        P(("exp", "tp"), None, None),
        P(("exp", "tp"), None, None),
    )
    out_specs = P(("exp", "tp"), None)
    return jax.shard_map(
        on_device, mesh=mesh, in_specs=in_specs, out_specs=out_specs, check_vma=False
    )
```

```python
import jax
import jax.numpy as jnp
from jax import lax
from jax.experimental import pallas as pl
from jax.experimental.pallas import tpu as pltpu
from jax.sharding import PartitionSpec as P

EPSILON = 1e-06
ROPE_BASE = 1000000.0
F32 = jnp.float32
BF16 = jnp.bfloat16
VMEM_BYTES = 48 * 1024 * 1024


def whole(count):
    return [pl.BlockSpec(memory_space=pltpu.VMEM)] * count


def shift(value, by):
    size = lax.axis_size("tp")
    return lax.ppermute(value, "tp", [(i, (i + by) % size) for i in range(size)])


def rope_tables(seq_len, head_dim):
    half_dim = head_dim // 2
    inv_freq = ROPE_BASE ** (-(jnp.arange(half_dim, dtype=F32) * 2.0) / head_dim)
    angles = jnp.arange(seq_len, dtype=F32)[:, None] * inv_freq[None, :]
    cos, sin = jnp.cos(angles), jnp.sin(angles)
    return jnp.concatenate([cos, cos], axis=1), jnp.concatenate([-sin, sin], axis=1)


def layer_kernel(*refs, first):
    order, own, left, right, opposite = refs[:5]
    refs = refs[5:]
    if first:
        past_keys, past_values = refs[:2]
        refs = refs[2:]
    (gain, w_q, w_k, w_v, w_o, q_gain, k_gain, cos, sin, seg_col, seg_row,
     to_right, to_left, to_opposite, to_own, keys_out, values_out,
     normed, queries, keys, values, context) = refs
    count, width = own.shape
    feat_dim = w_q.shape[0]
    head_dim = w_k.shape[1]
    heads = queries.shape[0]
    block = 128

    pieces = [piece[...].astype(F32) for piece in (own, left, right, opposite)]
    squares = sum(jnp.sum(piece * piece, axis=1, keepdims=True) for piece in pieces)
    scale = lax.rsqrt(squares / feat_dim + EPSILON)
    for place, piece in enumerate(pieces):
        at = order[place]
        columns = pl.ds(pl.multiple_of(at * width, width), width)
        normed[:, columns] = (piece * scale * gain[pl.ds(at, 1), :]).astype(BF16)

    here = pl.ds(first, count)
    turn_cos, turn_sin = cos[here, :], sin[here, :]

    def head_of(raw, head_gain):
        squares = jnp.mean(raw * raw, axis=1, keepdims=True)
        raw = raw * lax.rsqrt(squares + EPSILON) * head_gain[...]
        return (raw * turn_cos + pltpu.roll(raw, head_dim // 2, 1) * turn_sin).astype(BF16)

    if first:
        keys[:first, :] = past_keys[...]
        values[:first, :] = past_values[...]
    new_keys = head_of(jnp.dot(normed[...], w_k[...], preferred_element_type=F32), k_gain)
    new_values = jnp.dot(normed[...], w_v[...], preferred_element_type=F32).astype(BF16)
    keys[here, :] = new_keys
    values[here, :] = new_values
    keys_out[...] = new_keys
    values_out[...] = new_values
    for pair in range(heads // 2):
        raw = jnp.dot(
            normed[...], w_q[:, pl.ds(pair * 2 * head_dim, 2 * head_dim)],
            preferred_element_type=F32,
        )
        for one in range(2):
            queries[2 * pair + one] = head_of(raw[:, one * head_dim : (one + 1) * head_dim], q_gain)

    for start in range(0, count, block):
        span = first + start + block
        row_at = first + start + lax.broadcasted_iota(jnp.int32, (block, span), 0)
        col_at = lax.broadcasted_iota(jnp.int32, (block, span), 1)
        same = seg_col[pl.ds(first + start, block), :] == seg_row[:, :span]
        allowed = same & (col_at <= row_at)
        for head in range(heads):
            scores = lax.dot_general(
                queries[head, pl.ds(start, block), :], keys[:span, :], (((1,), (1,)), ((), ())),
                preferred_element_type=F32,
            ) * (float(head_dim) ** -0.5)
            scores = jnp.where(allowed, scores, -1e30)
            expo = jnp.exp(scores - jnp.max(scores, axis=1, keepdims=True))
            total = jnp.sum(expo, axis=1, keepdims=True)
            mixed = jnp.dot(expo.astype(BF16), values[:span, :], preferred_element_type=F32)
            context[pl.ds(start, block), pl.ds(head * head_dim, head_dim)] = (
                mixed / total
            ).astype(BF16)

    for place, out in ((2, to_right), (1, to_left), (3, to_opposite), (0, to_own)):
        columns = pl.ds(pl.multiple_of(order[place] * width, width), width)
        out[...] = jnp.dot(context[...], w_o[:, columns], preferred_element_type=F32).astype(BF16)


def run_layer(order, parts, past, first, gain, w_q, w_k, w_v, w_o, q_gain, k_gain, cos, sin, seg):
    count, width = parts[0].shape
    feat_dim = w_q.shape[0]
    head_dim = w_k.shape[1]
    heads = w_q.shape[1] // head_dim
    span = first + count
    piece = jax.ShapeDtypeStruct((count, width), BF16)
    kv = jax.ShapeDtypeStruct((count, head_dim), BF16)
    operands = [*parts, *past, gain, w_q, w_k, w_v, w_o, q_gain, k_gain, cos, sin, *seg]

    def kernel(*refs):
        layer_kernel(*refs, first=first)

    return pl.pallas_call(
        kernel,
        in_specs=[pl.BlockSpec(memory_space=pltpu.SMEM)] + whole(len(operands)),
        out_specs=whole(6),
        out_shape=(piece,) * 4 + (kv,) * 2,
        scratch_shapes=[
            pltpu.VMEM((count, feat_dim), BF16),
            pltpu.VMEM((heads, count, head_dim), BF16),
            pltpu.VMEM((span, head_dim), BF16),
            pltpu.VMEM((span, head_dim), BF16),
            pltpu.VMEM((count, heads * head_dim), BF16),
        ],
        compiler_params=pltpu.CompilerParams(vmem_limit_bytes=VMEM_BYTES),
        cost_estimate=pl.CostEstimate(
            flops=4 * count * feat_dim * (heads + 1) * head_dim
            + 4 * count * span * heads * head_dim,
            transcendentals=count * span * heads,
            bytes_accessed=4 * feat_dim * (heads + 1) * head_dim + 16 * count * width,
        ),
        name="layer",
    )(order, *operands)


def one_hot(places, cap):
    rows, tokens = places.shape
    slot = lax.broadcasted_iota(jnp.int32, (rows, cap, tokens), 1).astype(F32)
    return jnp.broadcast_to(places[:, None, :], slot.shape) == slot


def dispatch_kernel(columns, from_left, from_right, from_opposite, own, places, out, hidden, rounded):
    @pl.when(pl.program_id(0) == 0)
    def _():
        total = columns[...].astype(F32)
        for piece in (own, from_left, from_right, from_opposite):
            total = total + piece[...].astype(F32)
        hidden[...] = total
        rounded[...] = total.astype(BF16)

    blocks, group, tokens = places.shape
    cap = out.shape[1] // blocks
    for block in range(blocks):
        chosen = one_hot(places[block], cap).astype(F32).reshape(group * cap, tokens).astype(BF16)
        rows = jnp.dot(
            chosen, rounded[pl.ds(block * tokens, tokens), :], preferred_element_type=F32
        ).astype(BF16)
        out[:, pl.ds(block * cap, cap), :] = rows.reshape(group, cap, rows.shape[1])


def run_dispatch(columns, pieces, places, cap):
    count, width = columns.shape
    blocks, experts, tokens = places.shape
    group = 16
    fixed = pl.BlockSpec((count, width), lambda i: (0, 0))
    return pl.pallas_call(
        dispatch_kernel,
        grid=(experts // group,),
        in_specs=[fixed] * 5 + [pl.BlockSpec((blocks, group, tokens), lambda i: (0, i, 0))],
        out_specs=[pl.BlockSpec((group, blocks * cap, width), lambda i: (i, 0, 0)), fixed],
        out_shape=(
            jax.ShapeDtypeStruct((experts, blocks * cap, width), BF16),
            jax.ShapeDtypeStruct((count, width), F32),
        ),
        scratch_shapes=[pltpu.VMEM((count, width), BF16)],
        compiler_params=pltpu.CompilerParams(vmem_limit_bytes=VMEM_BYTES),
        cost_estimate=pl.CostEstimate(
            flops=2 * experts * cap * count * width, transcendentals=0,
            bytes_accessed=2 * experts * blocks * cap * width,
        ),
        name="dispatch",
    )(columns, *pieces, places)


def expert_kernel(rows, gain, w_gate_up, w_down, out, normed):
    groups, parts, slots, width = rows.shape
    count = groups * slots
    feat_dim = parts * width
    inner = w_down.shape[0]
    pieces = [rows[:, part].reshape(count, width).astype(F32) for part in range(parts)]
    squares = sum(jnp.sum(piece * piece, axis=1, keepdims=True) for piece in pieces)
    scale = lax.rsqrt(squares / feat_dim + EPSILON)
    for part, piece in enumerate(pieces):
        normed[:, pl.ds(part * width, width)] = (
            piece * scale * gain[pl.ds(part, 1), :]
        ).astype(BF16)
    both = jnp.dot(normed[...], w_gate_up[...], preferred_element_type=F32)
    gate, up = both[:, :inner], both[:, inner:]
    hidden = (gate * jax.nn.sigmoid(gate) * up).astype(BF16)
    for part in range(parts):
        result = jnp.dot(
            hidden, w_down[:, pl.ds(part * width, width)], preferred_element_type=F32
        )
        out[:, part] = result.astype(BF16).reshape(groups, slots, width)


def run_experts(arrived, gain, w_gate_up, w_down):
    sources, parts, slots, width = arrived.shape
    feat_dim, double = w_gate_up.shape
    groups = 8
    moving = pl.BlockSpec((groups, parts, slots, width), lambda i: (i, 0, 0, 0))

    def fixed(shape):
        return pl.BlockSpec(shape, lambda i: (0, 0), pipeline_mode=pl.Buffered(1))

    return pl.pallas_call(
        expert_kernel,
        grid=(sources // groups,),
        in_specs=[moving, fixed(gain.shape), fixed(w_gate_up.shape), fixed(w_down.shape)],
        out_specs=moving,
        out_shape=jax.ShapeDtypeStruct(arrived.shape, BF16),
        scratch_shapes=[pltpu.VMEM((groups * slots, feat_dim), BF16)],
        compiler_params=pltpu.CompilerParams(vmem_limit_bytes=VMEM_BYTES),
        cost_estimate=pl.CostEstimate(
            flops=3 * sources * slots * feat_dim * double,
            transcendentals=sources * slots * double // 2,
            bytes_accessed=4 * sources * slots * feat_dim + 3 * feat_dim * double,
        ),
        name="experts",
    )(arrived, gain, w_gate_up, w_down)


def combine_kernel(returned, gates, places, hidden, out, total):
    step = pl.program_id(0)

    @pl.when(step == 0)
    def _():
        total[...] = hidden[...]

    blocks, group, tokens = places.shape
    cap = returned.shape[1] // blocks
    for block in range(blocks):
        weights = jnp.where(
            one_hot(places[block], cap),
            jnp.broadcast_to(gates[block][:, None, :], (group, cap, tokens)),
            0.0,
        ).reshape(group * cap, tokens).astype(BF16)
        rows = returned[:, pl.ds(block * cap, cap), :].reshape(group * cap, -1)
        total[pl.ds(block * tokens, tokens), :] += lax.dot_general(
            weights, rows, (((0,), (0,)), ((), ())), preferred_element_type=F32
        )

    @pl.when(step == pl.num_programs(0) - 1)
    def _():
        out[...] = total[...].astype(BF16)


def run_combine(returned, gates, places, hidden):
    count, width = hidden.shape
    blocks, experts, tokens = places.shape
    group = 16
    table = pl.BlockSpec((blocks, group, tokens), lambda i: (0, i, 0))
    fixed = pl.BlockSpec((count, width), lambda i: (0, 0))
    return pl.pallas_call(
        combine_kernel,
        grid=(experts // group,),
        in_specs=[
            pl.BlockSpec((group, returned.shape[1], width), lambda i: (i, 0, 0)), table, table, fixed
        ],
        out_specs=fixed,
        out_shape=jax.ShapeDtypeStruct((count, width), BF16),
        scratch_shapes=[pltpu.VMEM((count, width), F32)],
        compiler_params=pltpu.CompilerParams(vmem_limit_bytes=VMEM_BYTES),
        cost_estimate=pl.CostEstimate(
            flops=2 * returned.size * tokens, transcendentals=0, bytes_accessed=2 * returned.size
        ),
        name="combine",
    )(returned, gates, places, hidden)


def join_kernel(order, own, left, right, opposite, out):
    width = own.shape[1]
    for place, piece in enumerate((own, left, right, opposite)):
        out[:, pl.ds(pl.multiple_of(order[place] * width, width), width)] = piece[...]


def run_join(order, pieces):
    count, width = pieces[0].shape
    return pl.pallas_call(
        join_kernel,
        in_specs=[pl.BlockSpec(memory_space=pltpu.SMEM)] + whole(4),
        out_specs=whole(1)[0],
        out_shape=jax.ShapeDtypeStruct((count, 4 * width), BF16),
        name="join",
    )(order, *pieces)


def on_device(
    audio_feats, w_audio, b_audio, segments, w_q, w_k, w_v, w_o, attn_gain, q_gain, k_gain,
    moe_gain, w_router, routes, w_gate_up, w_down,
):
    me = lax.axis_index("tp")
    tp_size = lax.axis_size("tp")
    tok_rows = audio_feats.shape[0]
    feat_dim = b_audio.shape[0]
    seq_len = segments.shape[1]
    head_dim = q_gain.shape[0]
    experts = w_router.shape[1]
    top_count = routes.shape[1]
    width = w_audio.shape[1]
    slot_cap = max(4, 2 * tok_rows * top_count // experts)
    order = lax.rem(me + jnp.array([0, 3, 1, 2], jnp.int32), tp_size)

    def exchange(value):
        return [value, shift(value, 1), shift(value, -1), shift(value, 2)]

    def in_order(value):
        stack = jnp.zeros((tp_size,) + value.shape, value.dtype)
        for place, piece in enumerate(exchange(value)):
            stack = lax.dynamic_update_slice_in_dim(stack, piece[None], order[place], 0)
        return stack

    seq_audio = in_order(audio_feats).reshape(seq_len, -1)

    expert_ids = jnp.arange(experts, dtype=jnp.int32)
    named = jnp.any(routes.T[:, None, :] == expert_ids[None, :, None], axis=0)
    token_ids = jnp.arange(tok_rows, dtype=jnp.int32)
    earlier = (token_ids[:, None] < token_ids[None, :]).astype(BF16)
    places = jnp.dot(named.astype(BF16), earlier, preferred_element_type=F32)
    places = in_order(jnp.where(named, places, -1.0).astype(BF16)).astype(F32)

    bias_part = lax.dynamic_slice_in_dim(b_audio, me * width, width, 0)
    columns = (jnp.dot(seq_audio, w_audio, preferred_element_type=F32) + bias_part).astype(BF16)

    cos, sin = rope_tables(seq_len, head_dim)
    seg = (segments.reshape(seq_len, 1), segments)
    router_part = lax.dynamic_slice_in_dim(w_router, me * width, width, 0)
    gain_part = lax.dynamic_slice_in_dim(moe_gain, me * width, width, 0)
    by_device = (tp_size, width)

    def gates_of(hidden, chunk_places):
        count = hidden.shape[0]
        blocks = chunk_places.shape[0]
        scaled = (hidden * gain_part).astype(BF16)
        partial = jnp.dot(scaled, router_part, preferred_element_type=F32)
        squares = jnp.sum(hidden * hidden, axis=1).reshape(blocks, tok_rows)
        squares = jnp.pad(squares, ((0, 8 - blocks), (0, 0)))
        packed = sum(exchange(jnp.concatenate([partial, squares], axis=0)))
        scale = lax.rsqrt(packed[count : count + blocks] / feat_dim + EPSILON)
        logits = packed[:count].reshape(blocks, tok_rows, experts).transpose(0, 2, 1)
        logits = logits * scale[:, None, :]
        here = chunk_places >= 0
        peak = jnp.max(jnp.where(here, logits, -jnp.inf), axis=1, keepdims=True)
        expo = jnp.where(here, jnp.exp(jnp.minimum(logits - peak, 0.0)), 0.0)
        gates = expo / jnp.sum(expo, axis=1, keepdims=True)
        return gates.astype(BF16).astype(F32)

    starts = (0, tok_rows, seq_len)
    past, pending = (), []
    for first, end in zip(starts[:-1], starts[1:]):
        chunk = columns[first:end]
        parts = exchange(chunk)
        *pieces, keys, values = run_layer(
            order, parts, past, first, attn_gain.reshape(by_device), w_q, w_k, w_v, w_o,
            q_gain[None], k_gain[None], cos, sin, seg,
        )
        past = (keys, values)
        to_right, to_left, to_opposite, mine = pieces
        summed = [shift(to_right, 1), shift(to_left, -1), shift(to_opposite, 2), mine]
        chunk_places = places[first // tok_rows : end // tok_rows]
        outgoing, hidden = run_dispatch(chunk, summed, chunk_places, slot_cap)
        arrived = lax.all_to_all(outgoing, ("exp", "tp"), 0, 0, tiled=True)
        pending.append((arrived, hidden, chunk_places))

    finished = []
    for arrived, hidden, chunk_places in pending:
        _, slots, _ = arrived.shape
        results = run_experts(
            arrived.reshape(-1, tp_size, slots, width), moe_gain.reshape(by_device),
            w_gate_up[0], w_down[0],
        )
        returned = lax.all_to_all(
            results.reshape(arrived.shape), ("exp", "tp"), 0, 0, tiled=True
        )
        gates = gates_of(hidden, chunk_places)
        finished.append(run_combine(returned, gates, chunk_places, hidden))

    blocks = jnp.concatenate(finished, axis=0).reshape(tp_size, tok_rows, width)

    def block_of(place):
        return lax.dynamic_index_in_dim(blocks, order[place], 0, keepdims=False)

    gathered = [
        block_of(0), shift(block_of(2), 1), shift(block_of(1), -1), shift(block_of(3), 2)
    ]
    return run_join(order, gathered)


def solution(mesh):
    in_specs = (
        P(("exp", "tp"), None),
        P(None, "tp"),
        P(),
        P("exp", None),
        P(None, "tp"),
        P(None, "tp"),
        P(None, "tp"),
        P("tp", None),
        P(),
        P(),
        P(),
        P(),
        P(),
        P(("exp", "tp"), None),
        P(("exp", "tp"), None, None),
        P(("exp", "tp"), None, None),
    )
    out_specs = P(("exp", "tp"), None)
    return jax.shard_map(
        on_device, mesh=mesh, in_specs=in_specs, out_specs=out_specs, check_vma=False
    )
```

```python
import jax
import jax.numpy as jnp
from jax import lax
from jax.experimental import pallas as pl
from jax.experimental.pallas import tpu as pltpu
from jax.sharding import PartitionSpec as P

EPSILON = 1e-06
ROPE_BASE = 1000000.0
F32 = jnp.float32
BF16 = jnp.bfloat16
VMEM_BYTES = 48 * 1024 * 1024


def whole(count):
    return [pl.BlockSpec(memory_space=pltpu.VMEM)] * count


def shift(value, by):
    size = lax.axis_size("tp")
    return lax.ppermute(value, "tp", [(i, (i + by) % size) for i in range(size)])


def rope_tables(seq_len, head_dim):
    half_dim = head_dim // 2
    inv_freq = ROPE_BASE ** (-(jnp.arange(half_dim, dtype=F32) * 2.0) / head_dim)
    angles = jnp.arange(seq_len, dtype=F32)[:, None] * inv_freq[None, :]
    cos, sin = jnp.cos(angles), jnp.sin(angles)
    return jnp.concatenate([cos, cos], axis=1), jnp.concatenate([-sin, sin], axis=1)


def qkv_kernel(
    order, own, left, right, top, bottom, gain, w_q, w_k, w_v, q_gain, k_gain, cos, sin,
    q_out, k_out, v_out, x_out, normed,
):
    seq_len, width = own.shape
    half = seq_len // 2
    feat_dim = w_q.shape[0]
    head_dim = w_k.shape[1]
    for part in range(2):
        rows = pl.ds(part * half, half)
        pieces = [own[rows, :], left[rows, :], right[rows, :], (bottom if part else top)[...]]
        pieces = [piece.astype(F32) for piece in pieces]
        squares = sum(jnp.sum(piece * piece, axis=1, keepdims=True) for piece in pieces)
        scale = lax.rsqrt(squares / feat_dim + EPSILON)
        for place, piece in enumerate(pieces):
            at = order[place]
            columns = pl.ds(pl.multiple_of(at * width, width), width)
            normed[rows, columns] = (piece * scale * gain[pl.ds(at, 1), :]).astype(BF16)

    def head(raw, head_gain):
        squares = jnp.mean(raw * raw, axis=1, keepdims=True)
        raw = raw * lax.rsqrt(squares + EPSILON) * head_gain[...]
        return (raw * cos[...] + pltpu.roll(raw, head_dim // 2, 1) * sin[...]).astype(BF16)

    blocks, heads, rows_each, _ = q_out.shape
    me = order[0]
    mine = pl.ds(pl.multiple_of(me * rows_each, rows_each), rows_each)
    for place, piece in enumerate((own, left, right)):
        x_out[:, pl.ds(pl.multiple_of(order[place] * width, width), width)] = piece[mine, :]
    opposite = pl.ds(pl.multiple_of(order[3] * width, width), width)
    for number in range(blocks):
        @pl.when(me == number)
        def _():
            source = top if number * rows_each < half else bottom
            x_out[:, opposite] = source[pl.ds(number * rows_each % half, rows_each), :]

    for pair in range(heads // 2):
        raw = jnp.dot(
            normed[...], w_q[:, pl.ds(pair * 2 * head_dim, 2 * head_dim)],
            preferred_element_type=F32,
        )
        for one in range(2):
            rotated = head(raw[:, one * head_dim : (one + 1) * head_dim], q_gain)
            q_out[:, 2 * pair + one] = rotated.reshape(blocks, rows_each, head_dim)
    k_out[...] = head(jnp.dot(normed[...], w_k[...], preferred_element_type=F32), k_gain)
    v_out[...] = jnp.dot(normed[...], w_v[...], preferred_element_type=F32).astype(BF16)


def attend_kernel(which, queries, keys, values, seg_col, seg_row, w_o, out, context):
    blocks, heads, rows_each, head_dim = queries.shape
    block = which[0]

    for number in range(blocks):

        @pl.when(block == number)
        def _():
            span = (number + 1) * rows_each
            first = number * rows_each
            row_at = first + lax.broadcasted_iota(jnp.int32, (rows_each, span), 0)
            col_at = lax.broadcasted_iota(jnp.int32, (rows_each, span), 1)
            allowed = (seg_col[pl.ds(first, rows_each), :] == seg_row[:, :span]) & (col_at <= row_at)
            for head in range(heads):
                scores = lax.dot_general(
                    queries[number, head], keys[:span, :], (((1,), (1,)), ((), ())),
                    preferred_element_type=F32,
                ) * (float(head_dim) ** -0.5)
                scores = jnp.where(allowed, scores, -1e30)
                expo = jnp.exp(scores - jnp.max(scores, axis=1, keepdims=True))
                total = jnp.sum(expo, axis=1, keepdims=True)
                mixed = jnp.dot(expo.astype(BF16), values[:span, :], preferred_element_type=F32)
                context[:, pl.ds(head * head_dim, head_dim)] = (mixed / total).astype(BF16)

    out[...] = jnp.dot(context[...], w_o[...], preferred_element_type=F32).astype(BF16)


def expert_kernel(rows, w_gate_up, w_down, out):
    width = w_down.shape[0]
    both = jnp.dot(rows[...], w_gate_up[...], preferred_element_type=F32)
    gate, up = both[:, :width], both[:, width:]
    hidden = (gate * jax.nn.sigmoid(gate) * up).astype(BF16)
    out[...] = jnp.dot(hidden, w_down[...], preferred_element_type=F32).astype(BF16)


def run_expert(rows, w_gate_up, w_down):
    count, feat_dim = rows.shape
    width = w_down.shape[0]
    block = 256
    return pl.pallas_call(
        expert_kernel,
        grid=(count // block,),
        in_specs=[
            pl.BlockSpec((block, feat_dim), lambda i: (i, 0)),
            pl.BlockSpec((feat_dim, 2 * width), lambda i: (0, 0)),
            pl.BlockSpec((width, feat_dim), lambda i: (0, 0)),
        ],
        out_specs=pl.BlockSpec((block, feat_dim), lambda i: (i, 0)),
        out_shape=jax.ShapeDtypeStruct((count, feat_dim), BF16),
        compiler_params=pltpu.CompilerParams(vmem_limit_bytes=VMEM_BYTES),
        cost_estimate=pl.CostEstimate(
            flops=6 * count * feat_dim * width, transcendentals=count * width,
            bytes_accessed=4 * count * feat_dim + 6 * feat_dim * width,
        ),
        name="experts",
    )(rows, w_gate_up, w_down)


def on_device(
    audio_feats, w_audio, b_audio, segments, w_q, w_k, w_v, w_o, attn_gain, q_gain, k_gain,
    moe_gain, w_router, routes, w_gate_up, w_down,
):
    me = lax.axis_index("tp")
    tp_size = lax.axis_size("tp")
    tok_rows = audio_feats.shape[0]
    feat_dim = b_audio.shape[0]
    seq_len = segments.shape[1]
    head_dim = q_gain.shape[0]
    experts = w_router.shape[1]
    top_count = routes.shape[1]
    heads = w_q.shape[1] // head_dim
    width = w_audio.shape[1]
    slot_cap = max(4, 2 * tok_rows * top_count // experts)
    parts = 2
    slots = experts * slot_cap // parts

    seq_audio = jnp.zeros((tp_size,) + audio_feats.shape, BF16)
    for by in range(tp_size):
        piece = shift(audio_feats, by) if by else audio_feats
        at = lax.rem(me - by + tp_size, tp_size)
        seq_audio = lax.dynamic_update_slice_in_dim(seq_audio, piece[None], at, 0)
    seq_audio = seq_audio.reshape(seq_len, -1)

    expert_ids = jnp.arange(experts, dtype=jnp.int32)
    named = jnp.any(routes[:, :, None] == expert_ids[None, None, :], axis=1)
    earlier = (
        jnp.arange(tok_rows)[None, :] < jnp.arange(tok_rows)[:, None]
    ).astype(BF16)
    places = jnp.dot(earlier, named.astype(BF16), preferred_element_type=F32)
    places = jnp.where(named, places, -1.0).astype(BF16)
    slot_no = jnp.arange(slot_cap, dtype=jnp.int32).astype(BF16)
    dispatch = (places.T[None, :, None, :] == slot_no.reshape(parts, 1, -1, 1)).astype(BF16)
    dispatch = dispatch.reshape(parts, -1, tok_rows)

    bias_part = lax.dynamic_slice_in_dim(b_audio, me * width, width, 0)
    columns = (jnp.dot(seq_audio, w_audio, preferred_element_type=F32) + bias_part).astype(BF16)
    half = seq_len // 2
    left = shift(columns, 1)
    right = shift(columns, -1)
    top = shift(left[:half], 1)
    bottom = shift(right[half:], -1)
    order = lax.rem(me + jnp.array([0, 3, 1, 2], jnp.int32), tp_size)

    cos, sin = rope_tables(seq_len, head_dim)
    queries, keys, values, x_mine = pl.pallas_call(
        qkv_kernel,
        in_specs=[pl.BlockSpec(memory_space=pltpu.SMEM)] + whole(13),
        out_specs=whole(4),
        out_shape=(
            jax.ShapeDtypeStruct((tp_size, heads, tok_rows, head_dim), BF16),
            jax.ShapeDtypeStruct((seq_len, head_dim), BF16),
            jax.ShapeDtypeStruct((seq_len, head_dim), BF16),
            jax.ShapeDtypeStruct((tok_rows, feat_dim), BF16),
        ),
        scratch_shapes=[pltpu.VMEM((seq_len, feat_dim), BF16)],
        compiler_params=pltpu.CompilerParams(vmem_limit_bytes=VMEM_BYTES),
        cost_estimate=pl.CostEstimate(
            flops=2 * seq_len * feat_dim * (heads + 2) * head_dim, transcendentals=seq_len * heads,
            bytes_accessed=2 * feat_dim * (seq_len + (heads + 2) * head_dim),
        ),
        name="project",
    )(
        order, columns, left, right, top, bottom, attn_gain.reshape(tp_size, width), w_q, w_k, w_v,
        q_gain[None], k_gain[None], cos, sin,
    )

    def attend(block):
        return pl.pallas_call(
            attend_kernel,
            in_specs=[pl.BlockSpec(memory_space=pltpu.SMEM)] + whole(6),
            out_specs=whole(1)[0],
            out_shape=jax.ShapeDtypeStruct((tok_rows, feat_dim), BF16),
            scratch_shapes=[pltpu.VMEM((tok_rows, heads * head_dim), BF16)],
            compiler_params=pltpu.CompilerParams(vmem_limit_bytes=VMEM_BYTES),
            cost_estimate=pl.CostEstimate(
                flops=2 * tok_rows * heads * head_dim * (2 * seq_len + feat_dim),
                transcendentals=tok_rows * heads * seq_len,
                bytes_accessed=2 * feat_dim * (heads * head_dim + tok_rows),
            ),
            name="attend",
        )(block[None], queries, keys, values, segments.reshape(seq_len, 1), segments, w_o)

    attn_out = None
    for by in (1, 3, 2, 0):
        piece = attend(lax.rem(me + by, tp_size))
        piece = (shift(piece, by) if by else piece).astype(F32)
        attn_out = piece if attn_out is None else attn_out + piece

    hidden_res = x_mine.astype(F32) + attn_out
    squares = jnp.mean(hidden_res * hidden_res, axis=-1, keepdims=True)
    normed = (hidden_res * lax.rsqrt(squares + EPSILON) * moe_gain).astype(BF16)

    def travel(rows):
        rows = rows.reshape(experts, -1, feat_dim)
        return lax.all_to_all(rows, ("exp", "tp"), 0, 0, tiled=True).reshape(-1, feat_dim)

    returned = []
    for part in range(parts):
        outgoing = jnp.dot(dispatch[part], normed, preferred_element_type=F32).astype(BF16)
        expert_out = run_expert(travel(outgoing), w_gate_up[0], w_down[0])
        returned.append(travel(expert_out))

    logits = jnp.dot(normed, w_router, preferred_element_type=F32)
    peak = jnp.max(jnp.where(named, logits, -jnp.inf), axis=1, keepdims=True)
    expo = jnp.where(named, jnp.exp(jnp.minimum(logits - peak, 0.0)), 0.0)
    gates = (expo / jnp.sum(expo, axis=1, keepdims=True)).astype(BF16)
    slot_of = jnp.arange(slots, dtype=jnp.int32)
    part_cap = slot_cap // parts
    spread = (expert_ids[:, None] == (slot_of // part_cap)[None, :]).astype(BF16)
    wide_gates = jnp.dot(gates, spread, preferred_element_type=F32)
    wide_places = jnp.dot(places, spread, preferred_element_type=F32)
    total = hidden_res
    for part in range(parts):
        slot = (slot_of % part_cap + part * part_cap).astype(F32)
        combine = jnp.where(wide_places == slot[None, :], wide_gates, 0.0).astype(BF16)
        total = total + jnp.dot(combine, returned[part], preferred_element_type=F32)
    return total.astype(BF16)


def solution(mesh):
    in_specs = (
        P(("exp", "tp"), None),
        P(None, "tp"),
        P(),
        P("exp", None),
        P(None, "tp"),
        P(None, "tp"),
        P(None, "tp"),
        P("tp", None),
        P(),
        P(),
        P(),
        P(),
        P(),
        P(("exp", "tp"), None),
        P(("exp", "tp"), None, None),
        P(("exp", "tp"), None, None),
    )
    out_specs = P(("exp", "tp"), None)
    return jax.shard_map(
        on_device, mesh=mesh, in_specs=in_specs, out_specs=out_specs, check_vma=False
    )
```

```python
import math

import jax
import jax.numpy as jnp
from jax import lax
from jax.experimental import pallas as pl
from jax.experimental.pallas import tpu as pltpu
from jax.sharding import PartitionSpec as P

EPSILON = 1e-06
ROPE_BASE = 1000000.0
F32 = jnp.float32
BF16 = jnp.bfloat16
VMEM_BYTES = 32 * 1024 * 1024
EXPERT_VMEM_BYTES = 56 * 1024 * 1024


def whole(count):
    return [pl.BlockSpec(memory_space=pltpu.VMEM)] * count


def far(count):
    return [pl.BlockSpec(memory_space=pltpu.HBM)] * count


def in_far(values):
    return [pltpu.with_memory_space_constraint(value, pltpu.HBM) for value in values]


def shift(value, by):
    size = lax.axis_size("tp")
    return lax.ppermute(value, "tp", [(i, (i + by) % size) for i in range(size)])


def rope_tables(seq_len, head_dim):
    half_dim = head_dim // 2
    inv_freq = ROPE_BASE ** (-(jnp.arange(half_dim, dtype=F32) * 2.0) / head_dim)
    angles = jnp.arange(seq_len, dtype=F32)[:, None] * inv_freq[None, :]
    cos, sin = jnp.cos(angles), jnp.sin(angles)
    return jnp.concatenate([cos, cos], axis=1), jnp.concatenate([-sin, sin], axis=1)


def columns_kernel(order, own, left, right, opposite, weight, bias, extra, first, second, near, sems):
    sources = (own, left, right, opposite)
    rows = own.shape[0]
    some = second.shape[0] // rows
    copies = [
        pltpu.make_async_copy(source, near.at[place], sems.at[place])
        for place, source in enumerate(sources)
    ]
    for copy in copies:
        copy.start()
    first[pl.ds(some * rows, extra.shape[0]), :] = extra[...]
    part = bias[pl.ds(order[0], 1), :]
    for place, copy in enumerate(copies):
        copy.wait()
        product = jnp.dot(near[place], weight[...], preferred_element_type=F32)
        product = (product + part).astype(BF16)
        at = order[place]
        for number in range(2 * some):
            out = (first, second)[number // some]

            @pl.when(at == number)
            def _():
                out[pl.ds(number % some * rows, rows), :] = product


def run_columns(order, pieces, weight, bias, extra):
    rows, depth = pieces[0].shape
    width = weight.shape[1]
    half = jax.ShapeDtypeStruct((2 * rows, width), BF16)
    longer = jax.ShapeDtypeStruct((2 * rows + extra.shape[0], width), BF16)
    return pl.pallas_call(
        columns_kernel,
        in_specs=[pl.BlockSpec(memory_space=pltpu.SMEM)] + far(4) + whole(3),
        out_specs=whole(2),
        out_shape=(longer, half),
        scratch_shapes=[pltpu.VMEM((4, rows, depth), BF16), pltpu.SemaphoreType.DMA((4,))],
        compiler_params=pltpu.CompilerParams(vmem_limit_bytes=VMEM_BYTES),
        cost_estimate=pl.CostEstimate(
            flops=8 * rows * weight.size, transcendentals=0,
            bytes_accessed=2 * weight.size + 8 * pieces[0].size,
        ),
        name="columns",
    )(order, *in_far(pieces), weight, bias, extra)


def chosen_kernel(order, own, left, right, opposite, first, second):
    experts, blocks, cap, columns = first.shape
    tokens = columns // blocks
    some = own.shape[0]
    slot = lax.broadcasted_iota(jnp.int32, (some, cap, tokens), 1).astype(F32)
    for place, piece in enumerate((own, left, right, opposite)):
        at = order[place]
        for number in range(2 * blocks):
            out = (first, second)[number // blocks]
            block = number % blocks

            @pl.when(at == number)
            def _():
                for part in range(experts // some):
                    places = piece[:, pl.ds(part * tokens, tokens)].astype(F32)
                    here = pl.ds(part * some, some)
                    met = jnp.broadcast_to(places[:, None, :], slot.shape) == slot
                    met = met.astype(F32).astype(BF16)
                    for other in range(blocks):
                        out[here, block, :, pl.ds(other * tokens, tokens)] = (
                            met if other == block else jnp.zeros_like(met)
                        )


def run_chosen(order, parts, tokens, experts, cap):
    rows, width = parts[0].shape
    some = experts * tokens // width
    table = pl.BlockSpec((some, width), lambda i: (rows // some - 1, 0))
    half = (experts, 2, cap, 2 * tokens)
    result = pl.BlockSpec(half, lambda i: (0, 0, 0, 0))
    return pl.pallas_call(
        chosen_kernel,
        grid=(1,),
        in_specs=[pl.BlockSpec(memory_space=pltpu.SMEM)] + [table] * 4,
        out_specs=[result] * 2,
        out_shape=(jax.ShapeDtypeStruct(half, BF16),) * 2,
        compiler_params=pltpu.CompilerParams(vmem_limit_bytes=VMEM_BYTES),
        name="chosen",
    )(order, *parts)


def layer_kernel(*refs, first):
    order, sources, refs = refs[0], refs[1:5], refs[5:]
    if first:
        past_keys, past_values = refs[:2]
        refs = refs[2:]
    weights, refs = refs[:4], refs[4:]
    (gain, q_gain, k_gain, cos, sin, seg_col, seg_row,
     to_right, to_left, to_opposite, to_own, keys_out, values_out,
     normed, queries, keys, values, context, near, w_k, w_v, w_q, w_o, sems) = refs
    count, width = to_own.shape
    feat_dim = w_q.shape[0]
    head_dim = w_k.shape[1]
    heads = queries.shape[0]
    block = 128
    factor = float(head_dim) ** -0.5 * math.log2(math.e)

    copies = [
        pltpu.make_async_copy(source.at[pl.ds(0, count), :], near.at[place], sems.at[place])
        for place, source in enumerate(sources)
    ] + [
        pltpu.make_async_copy(source, target, sems.at[4 + place])
        for place, (source, target) in enumerate(zip(weights, (w_k, w_v, w_q, w_o)))
    ]
    for copy in copies:
        copy.start()
    for copy in copies[:4]:
        copy.wait()

    pieces = [near[place].astype(F32) for place in range(4)]
    squares = sum(jnp.sum(piece * piece, axis=1, keepdims=True) for piece in pieces)
    scale = lax.rsqrt(squares / feat_dim + EPSILON)
    for place, piece in enumerate(pieces):
        at = order[place]
        columns = pl.ds(pl.multiple_of(at * width, width), width)
        normed[:, columns] = (piece * scale * gain[pl.ds(at, 1), :]).astype(BF16)

    here = pl.ds(first, count)
    turn_cos, turn_sin = cos[here, :], sin[here, :]

    def head_of(raw, head_gain):
        squares = jnp.mean(raw * raw, axis=1, keepdims=True)
        raw = raw * lax.rsqrt(squares + EPSILON) * head_gain[...]
        return (raw * turn_cos + pltpu.roll(raw, head_dim // 2, 1) * turn_sin).astype(BF16)

    if first:
        keys[:first, :] = past_keys[...]
        values[:first, :] = past_values[...]
    copies[4].wait()
    new_keys = head_of(jnp.dot(normed[...], w_k[...], preferred_element_type=F32), k_gain)
    copies[5].wait()
    new_values = jnp.dot(normed[...], w_v[...], preferred_element_type=F32).astype(BF16)
    keys[here, :] = new_keys
    values[here, :] = new_values
    keys_out[...] = new_keys
    values_out[...] = new_values
    copies[6].wait()
    for pair in range(heads // 2):
        raw = jnp.dot(
            normed[...], w_q[:, pl.ds(pair * 2 * head_dim, 2 * head_dim)],
            preferred_element_type=F32,
        )
        for one in range(2):
            queries[2 * pair + one] = head_of(raw[:, one * head_dim : (one + 1) * head_dim], q_gain)

    for start in range(0, count, block):
        span = first + start + block
        row_at = first + start + lax.broadcasted_iota(jnp.int32, (block, span), 0)
        col_at = lax.broadcasted_iota(jnp.int32, (block, span), 1)
        same = seg_col[pl.ds(first + start, block), :] == seg_row[:, :span]
        allowed = same & (col_at <= row_at)
        for head in range(heads):
            scores = lax.dot_general(
                queries[head, pl.ds(start, block), :], keys[:span, :], (((1,), (1,)), ((), ())),
                preferred_element_type=F32,
            )
            scores = jnp.where(allowed, scores, -1e30)
            expo = jnp.exp2((scores - jnp.max(scores, axis=1, keepdims=True)) * factor)
            total = jnp.sum(expo, axis=1, keepdims=True)
            mixed = jnp.dot(expo.astype(BF16), values[:span, :], preferred_element_type=F32)
            context[pl.ds(start, block), pl.ds(head * head_dim, head_dim)] = (
                mixed / total
            ).astype(BF16)

    copies[7].wait()
    for place, out in ((2, to_right), (1, to_left), (3, to_opposite), (0, to_own)):
        columns = pl.ds(pl.multiple_of(order[place] * width, width), width)
        out[...] = jnp.dot(context[...], w_o[:, columns], preferred_element_type=F32).astype(BF16)


def run_layer(
    order, parts, count, past, first, gain, w_q, w_k, w_v, w_o, q_gain, k_gain, cos, sin, seg
):
    width = parts[0].shape[1]
    feat_dim = w_q.shape[0]
    head_dim = w_k.shape[1]
    heads = w_q.shape[1] // head_dim
    span = first + count
    piece = jax.ShapeDtypeStruct((count, width), BF16)
    kv = jax.ShapeDtypeStruct((count, head_dim), BF16)
    weights = (w_k, w_v, w_q, w_o)
    operands = [*in_far(parts), *past, *in_far(weights), gain, q_gain, k_gain, cos, sin, *seg]

    def kernel(*refs):
        layer_kernel(*refs, first=first)

    return pl.pallas_call(
        kernel,
        in_specs=[pl.BlockSpec(memory_space=pltpu.SMEM)]
        + far(len(parts)) + whole(len(past)) + far(len(weights))
        + whole(len(operands) - len(parts) - len(past) - len(weights)),
        out_specs=whole(6),
        out_shape=(piece,) * 4 + (kv,) * 2,
        scratch_shapes=[
            pltpu.VMEM((count, feat_dim), BF16),
            pltpu.VMEM((heads, count, head_dim), BF16),
            pltpu.VMEM((span, head_dim), BF16),
            pltpu.VMEM((span, head_dim), BF16),
            pltpu.VMEM((count, heads * head_dim), BF16),
            pltpu.VMEM((len(parts), count, width), BF16),
        ]
        + [pltpu.VMEM(weight.shape, BF16) for weight in weights]
        + [pltpu.SemaphoreType.DMA((len(parts) + len(weights),))],
        compiler_params=pltpu.CompilerParams(vmem_limit_bytes=VMEM_BYTES),
        cost_estimate=pl.CostEstimate(
            flops=4 * count * feat_dim * (heads + 1) * head_dim
            + 4 * count * span * heads * head_dim,
            transcendentals=count * span * heads,
            bytes_accessed=4 * feat_dim * (heads + 1) * head_dim + 16 * count * width,
        ),
        name="layer",
    )(order, *operands)


def expert_kernel(rows, gain, w_gate_up, w_down, *rest):
    out, normed = rest[-2:]
    groups, parts, slots, width = rows.shape
    count = groups * slots
    feat_dim = parts * width
    inner = w_down.shape[0]
    pieces = [rows[:, part].reshape(count, width).astype(F32) for part in range(parts)]
    squares = sum(jnp.sum(piece * piece, axis=1, keepdims=True) for piece in pieces)
    scale = lax.rsqrt(squares / feat_dim + EPSILON)
    for part, piece in enumerate(pieces):
        normed[:, pl.ds(part * width, width)] = (
            piece * scale * gain[pl.ds(part, 1), :]
        ).astype(BF16)
    both = jnp.dot(normed[...], w_gate_up[...], preferred_element_type=F32)
    gate, up = both[:, :inner], both[:, inner:]
    hidden = (gate * jax.nn.sigmoid(gate) * up).astype(BF16)
    result = jnp.dot(hidden, w_down[...], preferred_element_type=F32)
    out[...] = result.astype(BF16).reshape(out.shape)


def run_experts(arrived, gain, w_gate_up, w_down, cap, chunk, earlier):
    sources, parts, slots, width = arrived.shape
    feat_dim, double = w_gate_up.shape
    groups = 8
    blocks = slots // cap

    def fixed(shape):
        return pl.BlockSpec(shape, lambda i: (0, 0), pipeline_mode=pl.Buffered(1))

    more = () if earlier is None else (earlier,)
    return pl.pallas_call(
        expert_kernel,
        grid=(sources // groups,),
        in_specs=[
            pl.BlockSpec((groups, parts, slots, width), lambda i: (i, 0, 0, 0)),
            fixed(gain.shape), fixed(w_gate_up.shape), fixed(w_down.shape),
        ] + [pl.BlockSpec(memory_space=pl.ANY)] * len(more),
        out_specs=pl.BlockSpec((groups, blocks, cap, feat_dim), lambda i: (i, chunk, 0, 0)),
        out_shape=pltpu.HBM((sources, parts, cap, feat_dim), BF16),
        scratch_shapes=[pltpu.VMEM((groups * slots, feat_dim), BF16)],
        input_output_aliases={4: 0} if more else {},
        compiler_params=pltpu.CompilerParams(vmem_limit_bytes=EXPERT_VMEM_BYTES),
        cost_estimate=pl.CostEstimate(
            flops=3 * sources * slots * feat_dim * double,
            transcendentals=sources * slots * double // 2,
            bytes_accessed=4 * sources * slots * feat_dim + 3 * feat_dim * double,
        ),
        name="experts",
    )(*in_far([arrived]), gain, *in_far([w_gate_up, w_down]), *more)


def join_kernel(order, own, left, right, opposite, out):
    width = own.shape[1]
    for place, piece in enumerate((own, left, right, opposite)):
        out[:, pl.ds(pl.multiple_of(order[place] * width, width), width)] = piece[...]


def run_join(order, pieces):
    count, width = pieces[0].shape
    return pl.pallas_call(
        join_kernel,
        in_specs=[pl.BlockSpec(memory_space=pltpu.SMEM)] + whole(4),
        out_specs=whole(1)[0],
        out_shape=jax.ShapeDtypeStruct((count, 4 * width), BF16),
        name="join",
    )(order, *pieces)


def on_device(
    audio_feats, w_audio, b_audio, segments, w_q, w_k, w_v, w_o, attn_gain, q_gain, k_gain,
    moe_gain, w_router, routes, w_gate_up, w_down,
):
    me = lax.axis_index("tp")
    tp_size = lax.axis_size("tp")
    tok_rows = audio_feats.shape[0]
    feat_dim = b_audio.shape[0]
    seq_len = segments.shape[1]
    head_dim = q_gain.shape[0]
    experts = w_router.shape[1]
    top_count = routes.shape[1]
    width = w_audio.shape[1]
    slot_cap = max(4, 2 * tok_rows * top_count // experts)
    order = lax.rem(me + jnp.array([0, 3, 1, 2], jnp.int32), tp_size)

    def exchange(value):
        return [value, shift(value, 1), shift(value, -1), shift(value, 2)]

    def in_order(value):
        stack = jnp.zeros((tp_size,) + value.shape, value.dtype)
        for place, piece in enumerate(exchange(value)):
            stack = lax.dynamic_update_slice_in_dim(stack, piece[None], order[place], 0)
        return stack

    expert_ids = jnp.arange(experts, dtype=jnp.int32)
    named = jnp.any(routes[:, :, None] == expert_ids[None, None, :], axis=1)
    token_ids = jnp.arange(tok_rows, dtype=jnp.int32)
    earlier = (token_ids[None, :] < token_ids[:, None]).astype(BF16)
    my_places = jnp.dot(earlier, named.astype(BF16), preferred_element_type=F32)
    my_places = jnp.where(named, my_places, -1.0).astype(BF16)
    groups = width // tok_rows
    extra = my_places.T.reshape(groups, -1, tok_rows).transpose(1, 0, 2).reshape(-1, width)

    chunk_a, chunk_b = run_columns(
        order, exchange(audio_feats), w_audio, b_audio.reshape(tp_size, width), extra
    )
    parts_a = exchange(chunk_a)
    chunk_b, _ = lax.optimization_barrier((chunk_b, parts_a[1]))
    parts_b = exchange(chunk_b)

    cos, sin = rope_tables(seq_len, head_dim)
    seg = (segments.reshape(seq_len, 1), segments)
    by_device = (tp_size, width)
    half = seq_len // 2

    def layer(first, parts, past):
        *pieces, keys, values = run_layer(
            order, parts, half, past, first, attn_gain.reshape(by_device), w_q, w_k, w_v, w_o,
            q_gain[None], k_gain[None], cos, sin, seg,
        )
        return pieces, (keys, values)

    def summands(pieces):
        to_right, to_left, to_opposite, mine = pieces
        return [shift(to_right, 1), shift(to_left, -1), shift(to_opposite, 2), mine]

    pieces_a, past = layer(0, parts_a, ())
    pieces_b, _ = layer(half, parts_b, past)
    tables, pieces_b = lax.optimization_barrier((parts_a, pieces_b))
    met = run_chosen(order, tables, tok_rows, experts, slot_cap)
    terms = (summands(pieces_a), summands(pieces_b))

    sent = []
    for number, (chunk, term) in enumerate(zip((chunk_a[:half], chunk_b), terms)):
        hidden = sum(piece.astype(F32) for piece in term) + chunk.astype(F32)
        hidden = hidden.astype(BF16)
        rows = jnp.dot(met[number].reshape(-1, half), hidden, preferred_element_type=F32).astype(BF16)
        sent.append((rows.reshape(experts, -1, width), hidden))
    first_rows, _ = lax.optimization_barrier((sent[0][0], terms[1]))
    results = None
    for number, rows in enumerate((first_rows, sent[1][0])):
        arrived = lax.all_to_all(rows, ("exp", "tp"), 0, 0, tiled=True)
        results = run_experts(
            arrived.reshape(-1, tp_size, rows.shape[1], width), moe_gain.reshape(by_device),
            w_gate_up[0], w_down[0], slot_cap, number, results,
        )
        if number == 0:
            halves, results = lax.optimization_barrier(([rows for _, rows in sent], results))
    blocks = jnp.concatenate(halves, axis=0)
    blocks = blocks.reshape(tp_size, tok_rows, width)

    def block_of(place):
        return lax.dynamic_index_in_dim(blocks, order[place], 0, keepdims=False)

    own = [block_of(0), shift(block_of(2), 1), shift(block_of(1), -1), shift(block_of(3), 2)]
    results, own = lax.optimization_barrier((results, own))
    hidden_res = run_join(order, own)
    hidden_res = hidden_res.astype(F32)
    returned = lax.all_to_all(
        results.reshape(experts, slot_cap, feat_dim), ("exp", "tp"), 0, 0, tiled=True
    )
    squares = jnp.mean(hidden_res * hidden_res, axis=-1, keepdims=True)
    normed = (hidden_res * lax.rsqrt(squares + EPSILON) * moe_gain).astype(BF16)

    logits = jnp.dot(normed, w_router, preferred_element_type=F32)
    peak = jnp.max(jnp.where(named, logits, -jnp.inf), axis=1, keepdims=True)
    expo = jnp.where(named, jnp.exp(jnp.minimum(logits - peak, 0.0)), 0.0)
    gates = (expo / jnp.sum(expo, axis=1, keepdims=True)).astype(BF16)
    slot_of = jnp.arange(experts * slot_cap, dtype=jnp.int32)
    spread = (expert_ids[:, None] == (slot_of // slot_cap)[None, :]).astype(BF16)
    wide_gates = jnp.dot(gates, spread, preferred_element_type=F32)
    wide_places = jnp.dot(my_places, spread, preferred_element_type=F32)
    combine = jnp.where(
        wide_places == (slot_of % slot_cap).astype(F32)[None, :], wide_gates, 0.0
    ).astype(BF16)
    moe_out = jnp.dot(
        combine, returned.reshape(experts * slot_cap, feat_dim), preferred_element_type=F32
    )
    return (hidden_res + moe_out).astype(BF16)


def solution(mesh):
    in_specs = (
        P(("exp", "tp"), None),
        P(None, "tp"),
        P(),
        P("exp", None),
        P(None, "tp"),
        P(None, "tp"),
        P(None, "tp"),
        P("tp", None),
        P(),
        P(),
        P(),
        P(),
        P(),
        P(("exp", "tp"), None),
        P(("exp", "tp"), None, None),
        P(("exp", "tp"), None, None),
    )
    out_specs = P(("exp", "tp"), None)
    return jax.shard_map(
        on_device, mesh=mesh, in_specs=in_specs, out_specs=out_specs, check_vma=False
    )
```

```python
import math

import jax
import jax.numpy as jnp
from jax import lax
from jax.experimental import pallas as pl
from jax.experimental.pallas import tpu as pltpu
from jax.sharding import PartitionSpec as P

EPSILON = 1e-06
ROPE_BASE = 1000000.0
F32 = jnp.float32
BF16 = jnp.bfloat16
VMEM_BYTES = 32 * 1024 * 1024
EXPERT_VMEM_BYTES = 56 * 1024 * 1024


def whole(count):
    return [pl.BlockSpec(memory_space=pltpu.VMEM)] * count


def far(count):
    return [pl.BlockSpec(memory_space=pltpu.HBM)] * count


def in_far(values):
    return [pltpu.with_memory_space_constraint(value, pltpu.HBM) for value in values]


def shift(value, by):
    size = lax.axis_size("tp")
    return lax.ppermute(value, "tp", [(i, (i + by) % size) for i in range(size)])


def rope_tables(seq_len, head_dim):
    half_dim = head_dim // 2
    inv_freq = ROPE_BASE ** (-(jnp.arange(half_dim, dtype=F32) * 2.0) / head_dim)
    angles = jnp.arange(seq_len, dtype=F32)[:, None] * inv_freq[None, :]
    cos, sin = jnp.cos(angles), jnp.sin(angles)
    return jnp.concatenate([cos, cos], axis=1), jnp.concatenate([-sin, sin], axis=1)


def columns_kernel(order, own, left, right, opposite, far_weight, bias, extra, first, second, near, weight, sems):
    sources = (own, left, right, opposite)
    rows = own.shape[0]
    some = second.shape[0] // rows
    copies = [
        pltpu.make_async_copy(source, near.at[place], sems.at[place])
        for place, source in enumerate(sources)
    ]
    last = pltpu.make_async_copy(far_weight, weight, sems.at[4])
    last.start()
    for copy in copies:
        copy.start()
    first[pl.ds(some * rows, extra.shape[0]), :] = extra[...]
    part = bias[pl.ds(order[0], 1), :]
    last.wait()
    for place, copy in enumerate(copies):
        copy.wait()
        product = jnp.dot(near[place], weight[...], preferred_element_type=F32)
        product = (product + part).astype(BF16)
        at = order[place]
        for number in range(2 * some):
            out = (first, second)[number // some]

            @pl.when(at == number)
            def _():
                out[pl.ds(number % some * rows, rows), :] = product


def run_columns(order, pieces, weight, bias, extra):
    rows, depth = pieces[0].shape
    width = weight.shape[1]
    half = jax.ShapeDtypeStruct((2 * rows, width), BF16)
    longer = jax.ShapeDtypeStruct((2 * rows + extra.shape[0], width), BF16)
    return pl.pallas_call(
        columns_kernel,
        in_specs=[pl.BlockSpec(memory_space=pltpu.SMEM)] + far(5) + whole(2),
        out_specs=whole(2),
        out_shape=(longer, half),
        scratch_shapes=[
            pltpu.VMEM((4, rows, depth), BF16),
            pltpu.VMEM(weight.shape, BF16),
            pltpu.SemaphoreType.DMA((5,)),
        ],
        compiler_params=pltpu.CompilerParams(vmem_limit_bytes=VMEM_BYTES),
        cost_estimate=pl.CostEstimate(
            flops=8 * rows * weight.size, transcendentals=0,
            bytes_accessed=2 * weight.size + 8 * pieces[0].size,
        ),
        name="columns",
    )(order, *in_far([*pieces, weight]), bias, extra)


def chosen_kernel(order, own, left, right, opposite, *outs):
    experts, pairs, rows, columns = outs[0].shape
    cap = rows // 2
    tokens = columns // (2 * pairs)
    some = own.shape[0]
    row = lax.broadcasted_iota(jnp.int32, (some, rows, tokens), 1)
    for place, piece in enumerate((own, left, right, opposite)):
        at = order[place]
        for number in range(2 * pairs):

            @pl.when(at == number)
            def _():
                here_columns = pl.ds(number * tokens, tokens)
                mine = (row // cap) == number % 2
                for part in range(experts // some):
                    places = piece[:, pl.ds(part * tokens, tokens)].astype(F32)
                    places = jnp.broadcast_to(places[:, None, :], row.shape)
                    here = pl.ds(part * some, some)
                    for which, out in enumerate(outs):
                        slot = jnp.where(mine, row % cap + which * cap, -2).astype(F32)
                        met = (places == slot).astype(F32).astype(BF16)
                        for pair in range(pairs):
                            out[here, pair, :, here_columns] = (
                                met if pair == number // 2 else jnp.zeros_like(met)
                            )


def run_chosen(order, parts, tokens, experts, cap, count):
    rows, width = parts[0].shape
    some = experts * tokens // width
    table = pl.BlockSpec((some, width), lambda i: (rows // some - 1, 0))
    shape = (experts, 2, 2 * cap // count, 4 * tokens)
    result = pl.BlockSpec(shape, lambda i: (0, 0, 0, 0))
    return pl.pallas_call(
        chosen_kernel,
        grid=(1,),
        in_specs=[pl.BlockSpec(memory_space=pltpu.SMEM)] + [table] * 4,
        out_specs=[result] * count,
        out_shape=(jax.ShapeDtypeStruct(shape, BF16),) * count,
        compiler_params=pltpu.CompilerParams(vmem_limit_bytes=VMEM_BYTES),
        name="chosen",
    )(order, *parts)


def layer_kernel(*refs, first):
    order, sources, refs = refs[0], refs[1:5], refs[5:]
    if first:
        past_keys, past_values = refs[:2]
        refs = refs[2:]
    weights, refs = refs[:4], refs[4:]
    (gain, q_gain, k_gain, cos, sin, seg_col, seg_row,
     to_right, to_left, to_opposite, to_own, keys_out, values_out,
     normed, queries, keys, values, context, near, w_k, w_v, w_q, w_o, sems) = refs
    count, width = to_own.shape
    feat_dim = w_q.shape[0]
    head_dim = w_k.shape[1]
    heads = queries.shape[0]
    block = 128
    factor = float(head_dim) ** -0.5 * math.log2(math.e)

    copies = [
        pltpu.make_async_copy(source.at[pl.ds(0, count), :], near.at[place], sems.at[place])
        for place, source in enumerate(sources)
    ] + [
        pltpu.make_async_copy(source, target, sems.at[4 + place])
        for place, (source, target) in enumerate(zip(weights, (w_k, w_v, w_q, w_o)))
    ]
    for copy in copies:
        copy.start()
    for copy in copies[:4]:
        copy.wait()

    pieces = [near[place].astype(F32) for place in range(4)]
    squares = sum(jnp.sum(piece * piece, axis=1, keepdims=True) for piece in pieces)
    scale = lax.rsqrt(squares / feat_dim + EPSILON)
    for place, piece in enumerate(pieces):
        at = order[place]
        columns = pl.ds(pl.multiple_of(at * width, width), width)
        normed[:, columns] = (piece * scale * gain[pl.ds(at, 1), :]).astype(BF16)

    here = pl.ds(first, count)
    turn_cos, turn_sin = cos[here, :], sin[here, :]

    def head_of(raw, head_gain):
        squares = jnp.mean(raw * raw, axis=1, keepdims=True)
        raw = raw * lax.rsqrt(squares + EPSILON) * head_gain[...]
        return (raw * turn_cos + pltpu.roll(raw, head_dim // 2, 1) * turn_sin).astype(BF16)

    if first:
        keys[:first, :] = past_keys[...]
        values[:first, :] = past_values[...]
    copies[4].wait()
    new_keys = head_of(jnp.dot(normed[...], w_k[...], preferred_element_type=F32), k_gain)
    copies[5].wait()
    new_values = jnp.dot(normed[...], w_v[...], preferred_element_type=F32).astype(BF16)
    keys[here, :] = new_keys
    values[here, :] = new_values
    keys_out[...] = new_keys
    values_out[...] = new_values
    copies[6].wait()
    for pair in range(heads // 2):
        raw = jnp.dot(
            normed[...], w_q[:, pl.ds(pair * 2 * head_dim, 2 * head_dim)],
            preferred_element_type=F32,
        )
        for one in range(2):
            queries[2 * pair + one] = head_of(raw[:, one * head_dim : (one + 1) * head_dim], q_gain)

    for start in range(0, count, block):
        span = first + start + block
        row_at = first + start + lax.broadcasted_iota(jnp.int32, (block, span), 0)
        col_at = lax.broadcasted_iota(jnp.int32, (block, span), 1)
        same = seg_col[pl.ds(first + start, block), :] == seg_row[:, :span]
        allowed = same & (col_at <= row_at)
        for head in range(heads):
            scores = lax.dot_general(
                queries[head, pl.ds(start, block), :], keys[:span, :], (((1,), (1,)), ((), ())),
                preferred_element_type=F32,
            )
            scores = jnp.where(allowed, scores, -1e30)
            expo = jnp.exp2((scores - jnp.max(scores, axis=1, keepdims=True)) * factor)
            total = jnp.sum(expo, axis=1, keepdims=True)
            mixed = jnp.dot(expo.astype(BF16), values[:span, :], preferred_element_type=F32)
            context[pl.ds(start, block), pl.ds(head * head_dim, head_dim)] = (
                mixed / total
            ).astype(BF16)

    copies[7].wait()
    for place, out in ((2, to_right), (1, to_left), (3, to_opposite), (0, to_own)):
        columns = pl.ds(pl.multiple_of(order[place] * width, width), width)
        out[...] = jnp.dot(context[...], w_o[:, columns], preferred_element_type=F32).astype(BF16)


def run_layer(
    order, parts, count, past, first, gain, w_q, w_k, w_v, w_o, q_gain, k_gain, cos, sin, seg
):
    width = parts[0].shape[1]
    feat_dim = w_q.shape[0]
    head_dim = w_k.shape[1]
    heads = w_q.shape[1] // head_dim
    span = first + count
    piece = jax.ShapeDtypeStruct((count, width), BF16)
    kv = jax.ShapeDtypeStruct((count, head_dim), BF16)
    weights = (w_k, w_v, w_q, w_o)
    operands = [*in_far(parts), *past, *in_far(weights), gain, q_gain, k_gain, cos, sin, *seg]

    def kernel(*refs):
        layer_kernel(*refs, first=first)

    return pl.pallas_call(
        kernel,
        in_specs=[pl.BlockSpec(memory_space=pltpu.SMEM)]
        + far(len(parts)) + whole(len(past)) + far(len(weights))
        + whole(len(operands) - len(parts) - len(past) - len(weights)),
        out_specs=whole(6),
        out_shape=(piece,) * 4 + (kv,) * 2,
        scratch_shapes=[
            pltpu.VMEM((count, feat_dim), BF16),
            pltpu.VMEM((heads, count, head_dim), BF16),
            pltpu.VMEM((span, head_dim), BF16),
            pltpu.VMEM((span, head_dim), BF16),
            pltpu.VMEM((count, heads * head_dim), BF16),
            pltpu.VMEM((len(parts), count, width), BF16),
        ]
        + [pltpu.VMEM(weight.shape, BF16) for weight in weights]
        + [pltpu.SemaphoreType.DMA((len(parts) + len(weights),))],
        compiler_params=pltpu.CompilerParams(vmem_limit_bytes=VMEM_BYTES),
        cost_estimate=pl.CostEstimate(
            flops=4 * count * feat_dim * (heads + 1) * head_dim
            + 4 * count * span * heads * head_dim,
            transcendentals=count * span * heads,
            bytes_accessed=4 * feat_dim * (heads + 1) * head_dim + 16 * count * width,
        ),
        name="layer",
    )(order, *operands)


def expert_kernel(rows, gain, w_gate_up, w_down, out, normed):
    groups, parts, slots, width = rows.shape
    count = groups * slots
    feat_dim = parts * width
    inner = w_down.shape[0]
    pieces = [rows[:, part].reshape(count, width).astype(F32) for part in range(parts)]
    squares = sum(jnp.sum(piece * piece, axis=1, keepdims=True) for piece in pieces)
    scale = lax.rsqrt(squares / feat_dim + EPSILON)
    for part, piece in enumerate(pieces):
        normed[:, pl.ds(part * width, width)] = (
            piece * scale * gain[pl.ds(part, 1), :]
        ).astype(BF16)
    both = jnp.dot(normed[...], w_gate_up[...], preferred_element_type=F32)
    gate, up = both[:, :inner], both[:, inner:]
    hidden = (gate * jax.nn.sigmoid(gate) * up).astype(BF16)
    result = jnp.dot(hidden, w_down[...], preferred_element_type=F32)
    out[...] = result.astype(BF16)


def run_experts(arrived, gain, w_gate_up, w_down):
    sources, parts, slots, width = arrived.shape
    feat_dim, double = w_gate_up.shape
    groups = 8

    def fixed(shape):
        return pl.BlockSpec(shape, lambda i: (0, 0), pipeline_mode=pl.Buffered(1))

    return pl.pallas_call(
        expert_kernel,
        grid=(sources // groups,),
        in_specs=[
            pl.BlockSpec((groups, parts, slots, width), lambda i: (i, 0, 0, 0)),
            fixed(gain.shape), fixed(w_gate_up.shape), fixed(w_down.shape),
        ],
        out_specs=pl.BlockSpec((groups * slots, feat_dim), lambda i: (i, 0)),
        out_shape=pltpu.HBM((sources * slots, feat_dim), BF16),
        scratch_shapes=[pltpu.VMEM((groups * slots, feat_dim), BF16)],
        compiler_params=pltpu.CompilerParams(vmem_limit_bytes=EXPERT_VMEM_BYTES),
        cost_estimate=pl.CostEstimate(
            flops=3 * sources * slots * feat_dim * double,
            transcendentals=sources * slots * double // 2,
            bytes_accessed=4 * sources * slots * feat_dim + 3 * feat_dim * double,
        ),
        name="experts",
    )(*in_far([arrived]), gain, *in_far([w_gate_up, w_down]))


def join_kernel(order, own, left, right, opposite, out):
    width = own.shape[1]
    for place, piece in enumerate((own, left, right, opposite)):
        out[:, pl.ds(pl.multiple_of(order[place] * width, width), width)] = piece[...]


def run_join(order, pieces):
    count, width = pieces[0].shape
    return pl.pallas_call(
        join_kernel,
        in_specs=[pl.BlockSpec(memory_space=pltpu.SMEM)] + whole(4),
        out_specs=whole(1)[0],
        out_shape=jax.ShapeDtypeStruct((count, 4 * width), BF16),
        name="join",
    )(order, *pieces)


def on_device(
    audio_feats, w_audio, b_audio, segments, w_q, w_k, w_v, w_o, attn_gain, q_gain, k_gain,
    moe_gain, w_router, routes, w_gate_up, w_down,
):
    me = lax.axis_index("tp")
    tp_size = lax.axis_size("tp")
    tok_rows = audio_feats.shape[0]
    feat_dim = b_audio.shape[0]
    seq_len = segments.shape[1]
    head_dim = q_gain.shape[0]
    experts = w_router.shape[1]
    top_count = routes.shape[1]
    width = w_audio.shape[1]
    slot_cap = max(4, 2 * tok_rows * top_count // experts)
    order = lax.rem(me + jnp.array([0, 3, 1, 2], jnp.int32), tp_size)

    def exchange(value):
        return [value, shift(value, 1), shift(value, -1), shift(value, 2)]

    def in_order(value):
        stack = jnp.zeros((tp_size,) + value.shape, value.dtype)
        for place, piece in enumerate(exchange(value)):
            stack = lax.dynamic_update_slice_in_dim(stack, piece[None], order[place], 0)
        return stack

    expert_ids = jnp.arange(experts, dtype=jnp.int32)
    named = jnp.any(routes[:, :, None] == expert_ids[None, None, :], axis=1)
    token_ids = jnp.arange(tok_rows, dtype=jnp.int32)
    earlier = (token_ids[None, :] < token_ids[:, None]).astype(BF16)
    my_places = jnp.dot(earlier, named.astype(BF16), preferred_element_type=F32)
    my_places = jnp.where(named, my_places, -1.0).astype(BF16)
    groups = width // tok_rows
    extra = my_places.T.reshape(groups, -1, tok_rows).transpose(1, 0, 2).reshape(-1, width)

    chunk_a, chunk_b = run_columns(
        order, exchange(audio_feats), w_audio, b_audio.reshape(tp_size, width), extra
    )
    parts_a = exchange(chunk_a)
    chunk_b, _ = lax.optimization_barrier((chunk_b, parts_a[1]))
    parts_b = exchange(chunk_b)

    cos, sin = rope_tables(seq_len, head_dim)
    seg = (segments.reshape(seq_len, 1), segments)
    by_device = (tp_size, width)
    half = seq_len // 2

    def layer(first, parts, past):
        *pieces, keys, values = run_layer(
            order, parts, half, past, first, attn_gain.reshape(by_device), w_q, w_k, w_v, w_o,
            q_gain[None], k_gain[None], cos, sin, seg,
        )
        return pieces, (keys, values)

    def summands(pieces):
        to_right, to_left, to_opposite, mine = pieces
        return [shift(to_right, 1), shift(to_left, -1), shift(to_opposite, 2), mine]

    pieces_a, past = layer(0, parts_a, ())
    pieces_b, _ = layer(half, parts_b, past)
    tables, pieces_b = lax.optimization_barrier((parts_a, pieces_b))
    count = 2
    met = run_chosen(order, tables, tok_rows, experts, slot_cap, count)
    terms = (summands(pieces_a), summands(pieces_b))
    blocks = jnp.concatenate(
        [
            (sum(piece.astype(F32) for piece in term) + chunk.astype(F32)).astype(BF16)
            for chunk, term in zip((chunk_a[:half], chunk_b), terms)
        ],
        axis=0,
    )

    def travel(rows):
        return lax.all_to_all(rows, ("exp", "tp"), 0, 0, tiled=True)

    results = []
    for chosen in met:
        rows = jnp.dot(chosen.reshape(-1, seq_len), blocks, preferred_element_type=F32)
        arrived = travel(rows.astype(BF16).reshape(experts, -1, width))
        results.append(
            run_experts(
                arrived.reshape(-1, tp_size, arrived.shape[1], width),
                moe_gain.reshape(by_device), w_gate_up[0], w_down[0],
            ).reshape(experts, -1, feat_dim)
        )

    blocks, _ = lax.optimization_barrier((blocks, results[0]))
    blocks = blocks.reshape(tp_size, tok_rows, width)

    def block_of(place):
        return lax.dynamic_index_in_dim(blocks, order[place], 0, keepdims=False)

    own = [block_of(0), shift(block_of(2), 1), shift(block_of(1), -1), shift(block_of(3), 2)]
    results[1], own = lax.optimization_barrier((results[1], own))
    hidden_res = run_join(order, own)
    hidden_res = hidden_res.astype(F32)
    returned = [travel(rows).reshape(-1, feat_dim) for rows in results]
    squares = jnp.mean(hidden_res * hidden_res, axis=-1, keepdims=True)
    normed = (hidden_res * lax.rsqrt(squares + EPSILON) * moe_gain).astype(BF16)

    logits = jnp.dot(normed, w_router, preferred_element_type=F32)
    peak = jnp.max(jnp.where(named, logits, -jnp.inf), axis=1, keepdims=True)
    expo = jnp.where(named, jnp.exp(jnp.minimum(logits - peak, 0.0)), 0.0)
    gates = (expo / jnp.sum(expo, axis=1, keepdims=True)).astype(BF16)
    part_cap = slot_cap // count
    slot_of = jnp.arange(experts * part_cap, dtype=jnp.int32)
    spread = (expert_ids[:, None] == (slot_of // part_cap)[None, :]).astype(BF16)
    wide_gates = jnp.dot(gates, spread, preferred_element_type=F32)
    wide_places = jnp.dot(my_places, spread, preferred_element_type=F32)
    total = hidden_res
    for part in range(count):
        slot = (slot_of % part_cap + part * part_cap).astype(F32)
        combine = jnp.where(wide_places == slot[None, :], wide_gates, 0.0).astype(BF16)
        total = total + jnp.dot(combine, returned[part], preferred_element_type=F32)
    return total.astype(BF16)


def solution(mesh):
    in_specs = (
        P(("exp", "tp"), None),
        P(None, "tp"),
        P(),
        P("exp", None),
        P(None, "tp"),
        P(None, "tp"),
        P(None, "tp"),
        P("tp", None),
        P(),
        P(),
        P(),
        P(),
        P(),
        P(("exp", "tp"), None),
        P(("exp", "tp"), None, None),
        P(("exp", "tp"), None, None),
    )
    out_specs = P(("exp", "tp"), None)
    return jax.shard_map(
        on_device, mesh=mesh, in_specs=in_specs, out_specs=out_specs, check_vma=False
    )
```

```python
import math

import jax
import jax.numpy as jnp
from jax import lax
from jax.experimental import pallas as pl
from jax.experimental.pallas import tpu as pltpu
from jax.sharding import PartitionSpec as P

EPSILON = 1e-06
ROPE_BASE = 1000000.0
F32 = jnp.float32
BF16 = jnp.bfloat16
VMEM_BYTES = 32 * 1024 * 1024
EXPERT_VMEM_BYTES = 56 * 1024 * 1024


def whole(count):
    return [pl.BlockSpec(memory_space=pltpu.VMEM)] * count


def far(count):
    return [pl.BlockSpec(memory_space=pltpu.HBM)] * count


def in_far(values):
    return [pltpu.with_memory_space_constraint(value, pltpu.HBM) for value in values]


def shift(value, by):
    size = lax.axis_size("tp")
    return lax.ppermute(value, "tp", [(i, (i + by) % size) for i in range(size)])


def rope_tables(seq_len, head_dim):
    half_dim = head_dim // 2
    inv_freq = ROPE_BASE ** (-(jnp.arange(half_dim, dtype=F32) * 2.0) / head_dim)
    angles = jnp.arange(seq_len, dtype=F32)[:, None] * inv_freq[None, :]
    cos, sin = jnp.cos(angles), jnp.sin(angles)
    return jnp.concatenate([cos, cos], axis=1), jnp.concatenate([-sin, sin], axis=1)


def columns_kernel(order, own, left, right, opposite, far_weight, bias, extra, first, second, near, weight, sems):
    sources = (own, left, right, opposite)
    rows = own.shape[0]
    some = second.shape[0] // rows
    copies = [
        pltpu.make_async_copy(source, near.at[place], sems.at[place])
        for place, source in enumerate(sources)
    ]
    last = pltpu.make_async_copy(far_weight, weight, sems.at[4])
    last.start()
    for copy in copies:
        copy.start()
    first[pl.ds(some * rows, extra.shape[0]), :] = extra[...]
    part = bias[pl.ds(order[0], 1), :]
    last.wait()
    for place, copy in enumerate(copies):
        copy.wait()
        product = jnp.dot(near[place], weight[...], preferred_element_type=F32)
        product = (product + part).astype(BF16)
        at = order[place]
        for number in range(2 * some):
            out = (first, second)[number // some]

            @pl.when(at == number)
            def _():
                out[pl.ds(number % some * rows, rows), :] = product


def run_columns(order, pieces, weight, bias, extra):
    rows, depth = pieces[0].shape
    width = weight.shape[1]
    half = jax.ShapeDtypeStruct((2 * rows, width), BF16)
    longer = jax.ShapeDtypeStruct((2 * rows + extra.shape[0], width), BF16)
    return pl.pallas_call(
        columns_kernel,
        in_specs=[pl.BlockSpec(memory_space=pltpu.SMEM)] + far(5) + whole(2),
        out_specs=whole(2),
        out_shape=(longer, half),
        scratch_shapes=[
            pltpu.VMEM((4, rows, depth), BF16),
            pltpu.VMEM(weight.shape, BF16),
            pltpu.SemaphoreType.DMA((5,)),
        ],
        compiler_params=pltpu.CompilerParams(vmem_limit_bytes=VMEM_BYTES),
        cost_estimate=pl.CostEstimate(
            flops=8 * rows * weight.size, transcendentals=0,
            bytes_accessed=2 * weight.size + 8 * pieces[0].size,
        ),
        name="columns",
    )(order, *in_far(pieces[:1]), *pieces[1:], *in_far([weight]), bias, extra)


def chosen_kernel(order, own, left, right, opposite, *outs):
    experts, pairs, rows, columns = outs[0].shape
    cap = rows // 2
    tokens = columns // (2 * pairs)
    some = own.shape[0]
    row = lax.broadcasted_iota(jnp.int32, (some, rows, tokens), 1)
    for place, piece in enumerate((own, left, right, opposite)):
        at = order[place]
        for number in range(2 * pairs):

            @pl.when(at == number)
            def _():
                here_columns = pl.ds(number * tokens, tokens)
                mine = (row // cap) == number % 2
                for part in range(experts // some):
                    places = piece[:, pl.ds(part * tokens, tokens)].astype(F32)
                    places = jnp.broadcast_to(places[:, None, :], row.shape)
                    here = pl.ds(part * some, some)
                    for which, out in enumerate(outs):
                        slot = jnp.where(mine, row % cap + which * cap, -2).astype(F32)
                        met = (places == slot).astype(F32).astype(BF16)
                        for pair in range(pairs):
                            out[here, pair, :, here_columns] = (
                                met if pair == number // 2 else jnp.zeros_like(met)
                            )


def run_chosen(order, parts, tokens, experts, cap, count):
    rows, width = parts[0].shape
    some = experts * tokens // width
    table = pl.BlockSpec((some, width), lambda i: (rows // some - 1, 0))
    shape = (experts, 2, 2 * cap // count, 4 * tokens)
    result = pl.BlockSpec(shape, lambda i: (0, 0, 0, 0))
    return pl.pallas_call(
        chosen_kernel,
        grid=(1,),
        in_specs=[pl.BlockSpec(memory_space=pltpu.SMEM)] + [table] * 4,
        out_specs=[result] * count,
        out_shape=(jax.ShapeDtypeStruct(shape, BF16),) * count,
        compiler_params=pltpu.CompilerParams(vmem_limit_bytes=VMEM_BYTES),
        name="chosen",
    )(order, *parts)


def layer_kernel(*refs, first):
    order, sources, refs = refs[0], refs[1:5], refs[5:]
    if first:
        past_keys, past_values = refs[:2]
        refs = refs[2:]
    weights, refs = refs[:4], refs[4:]
    (gain, q_gain, k_gain, cos, sin, seg_col, seg_row,
     to_right, to_left, to_opposite, to_own, keys_out, values_out,
     normed, queries, keys, values, context, near, w_k, w_v, w_q, w_o, sems) = refs
    count, width = to_own.shape
    feat_dim = w_q.shape[0]
    head_dim = w_k.shape[1]
    heads = queries.shape[0]
    block = 128
    factor = float(head_dim) ** -0.5 * math.log2(math.e)

    copies = [
        pltpu.make_async_copy(source.at[pl.ds(0, count), :], near.at[place], sems.at[place])
        for place, source in enumerate(sources)
    ] + [
        pltpu.make_async_copy(source, target, sems.at[4 + place])
        for place, (source, target) in enumerate(zip(weights, (w_k, w_v, w_q, w_o)))
    ]
    for copy in copies:
        copy.start()
    for copy in copies[:4]:
        copy.wait()

    pieces = [near[place].astype(F32) for place in range(4)]
    squares = sum(jnp.sum(piece * piece, axis=1, keepdims=True) for piece in pieces)
    scale = lax.rsqrt(squares / feat_dim + EPSILON)
    for place, piece in enumerate(pieces):
        at = order[place]
        columns = pl.ds(pl.multiple_of(at * width, width), width)
        normed[:, columns] = (piece * scale * gain[:, columns]).astype(BF16)

    here = pl.ds(first, count)
    turn_cos, turn_sin = cos[here, :], sin[here, :]

    def head_of(raw, head_gain):
        squares = jnp.mean(raw * raw, axis=1, keepdims=True)
        raw = raw * lax.rsqrt(squares + EPSILON) * head_gain[...]
        return (raw * turn_cos + pltpu.roll(raw, head_dim // 2, 1) * turn_sin).astype(BF16)

    if first:
        keys[:first, :] = past_keys[...]
        values[:first, :] = past_values[...]
    copies[4].wait()
    new_keys = head_of(jnp.dot(normed[...], w_k[...], preferred_element_type=F32), k_gain)
    copies[5].wait()
    new_values = jnp.dot(normed[...], w_v[...], preferred_element_type=F32).astype(BF16)
    keys[here, :] = new_keys
    values[here, :] = new_values
    keys_out[...] = new_keys
    values_out[...] = new_values
    copies[6].wait()
    for pair in range(heads // 2):
        raw = jnp.dot(
            normed[...], w_q[:, pl.ds(pair * 2 * head_dim, 2 * head_dim)],
            preferred_element_type=F32,
        )
        for one in range(2):
            queries[2 * pair + one] = head_of(raw[:, one * head_dim : (one + 1) * head_dim], q_gain)

    for start in range(0, count, block):
        span = first + start + block
        row_at = first + start + lax.broadcasted_iota(jnp.int32, (block, span), 0)
        col_at = lax.broadcasted_iota(jnp.int32, (block, span), 1)
        same = seg_col[pl.ds(first + start, block), :] == seg_row[:, :span]
        allowed = same & (col_at <= row_at)
        for head in range(heads):
            scores = lax.dot_general(
                queries[head, pl.ds(start, block), :], keys[:span, :], (((1,), (1,)), ((), ())),
                preferred_element_type=F32,
            )
            scores = jnp.where(allowed, scores, -1e30)
            expo = jnp.exp2((scores - jnp.max(scores, axis=1, keepdims=True)) * factor)
            total = jnp.sum(expo, axis=1, keepdims=True)
            mixed = jnp.dot(expo.astype(BF16), values[:span, :], preferred_element_type=F32)
            context[pl.ds(start, block), pl.ds(head * head_dim, head_dim)] = (
                mixed / total
            ).astype(BF16)

    copies[7].wait()
    for place, out in ((2, to_right), (1, to_left), (3, to_opposite), (0, to_own)):
        columns = pl.ds(pl.multiple_of(order[place] * width, width), width)
        out[...] = jnp.dot(context[...], w_o[:, columns], preferred_element_type=F32).astype(BF16)


def run_layer(
    order, parts, count, past, first, gain, w_q, w_k, w_v, w_o, q_gain, k_gain, cos, sin, seg
):
    width = parts[0].shape[1]
    feat_dim = w_q.shape[0]
    head_dim = w_k.shape[1]
    heads = w_q.shape[1] // head_dim
    span = first + count
    piece = jax.ShapeDtypeStruct((count, width), BF16)
    kv = jax.ShapeDtypeStruct((count, head_dim), BF16)
    weights = (w_k, w_v, w_q, w_o)
    operands = [*parts, *past, *in_far(weights), gain, q_gain, k_gain, cos, sin, *seg]

    def kernel(*refs):
        layer_kernel(*refs, first=first)

    return pl.pallas_call(
        kernel,
        in_specs=[pl.BlockSpec(memory_space=pltpu.SMEM)]
        + far(len(parts)) + whole(len(past)) + far(len(weights))
        + whole(len(operands) - len(parts) - len(past) - len(weights)),
        out_specs=whole(6),
        out_shape=(piece,) * 4 + (kv,) * 2,
        scratch_shapes=[
            pltpu.VMEM((count, feat_dim), BF16),
            pltpu.VMEM((heads, count, head_dim), BF16),
            pltpu.VMEM((span, head_dim), BF16),
            pltpu.VMEM((span, head_dim), BF16),
            pltpu.VMEM((count, heads * head_dim), BF16),
            pltpu.VMEM((len(parts), count, width), BF16),
        ]
        + [pltpu.VMEM(weight.shape, BF16) for weight in weights]
        + [pltpu.SemaphoreType.DMA((len(parts) + len(weights),))],
        compiler_params=pltpu.CompilerParams(vmem_limit_bytes=VMEM_BYTES),
        cost_estimate=pl.CostEstimate(
            flops=4 * count * feat_dim * (heads + 1) * head_dim
            + 4 * count * span * heads * head_dim,
            transcendentals=count * span * heads,
            bytes_accessed=4 * feat_dim * (heads + 1) * head_dim + 16 * count * width,
        ),
        name="layer",
    )(order, *operands)


def expert_kernel(rows, gain, w_gate_up, w_down, out, normed):
    groups, parts, slots, width = rows.shape
    count = groups * slots
    feat_dim = parts * width
    inner = w_down.shape[0]
    pieces = [rows[:, part].reshape(count, width).astype(F32) for part in range(parts)]
    squares = sum(jnp.sum(piece * piece, axis=1, keepdims=True) for piece in pieces)
    scale = lax.rsqrt(squares / feat_dim + EPSILON)
    for part, piece in enumerate(pieces):
        normed[:, pl.ds(part * width, width)] = (
            piece * scale * gain[pl.ds(part, 1), :]
        ).astype(BF16)
    both = jnp.dot(normed[...], w_gate_up[...], preferred_element_type=F32)
    gate, up = both[:, :inner], both[:, inner:]
    hidden = (gate * jax.nn.sigmoid(gate) * up).astype(BF16)
    result = jnp.dot(hidden, w_down[...], preferred_element_type=F32)
    out[...] = result.astype(BF16)


def run_experts(arrived, gain, w_gate_up, w_down):
    sources, parts, slots, width = arrived.shape
    feat_dim, double = w_gate_up.shape
    groups = 8

    def fixed(shape):
        return pl.BlockSpec(shape, lambda i: (0, 0), pipeline_mode=pl.Buffered(1))

    return pl.pallas_call(
        expert_kernel,
        grid=(sources // groups,),
        in_specs=[
            pl.BlockSpec((groups, parts, slots, width), lambda i: (i, 0, 0, 0)),
            fixed(gain.shape), fixed(w_gate_up.shape), fixed(w_down.shape),
        ],
        out_specs=pl.BlockSpec((groups * slots, feat_dim), lambda i: (i, 0)),
        out_shape=pltpu.HBM((sources * slots, feat_dim), BF16),
        scratch_shapes=[pltpu.VMEM((groups * slots, feat_dim), BF16)],
        compiler_params=pltpu.CompilerParams(vmem_limit_bytes=EXPERT_VMEM_BYTES),
        cost_estimate=pl.CostEstimate(
            flops=3 * sources * slots * feat_dim * double,
            transcendentals=sources * slots * double // 2,
            bytes_accessed=4 * sources * slots * feat_dim + 3 * feat_dim * double,
        ),
        name="experts",
    )(*in_far([arrived]), gain, *in_far([w_gate_up, w_down]))


def join_kernel(order, own, left, right, opposite, out):
    width = own.shape[1]
    for place, piece in enumerate((own, left, right, opposite)):
        out[:, pl.ds(pl.multiple_of(order[place] * width, width), width)] = piece[...]


def run_join(order, pieces):
    count, width = pieces[0].shape
    return pl.pallas_call(
        join_kernel,
        in_specs=[pl.BlockSpec(memory_space=pltpu.SMEM)] + whole(4),
        out_specs=whole(1)[0],
        out_shape=jax.ShapeDtypeStruct((count, 4 * width), BF16),
        name="join",
    )(order, *pieces)


def on_device(
    audio_feats, w_audio, b_audio, segments, w_q, w_k, w_v, w_o, attn_gain, q_gain, k_gain,
    moe_gain, w_router, routes, w_gate_up, w_down,
):
    me = lax.axis_index("tp")
    tp_size = lax.axis_size("tp")
    tok_rows = audio_feats.shape[0]
    feat_dim = b_audio.shape[0]
    seq_len = segments.shape[1]
    head_dim = q_gain.shape[0]
    experts = w_router.shape[1]
    top_count = routes.shape[1]
    width = w_audio.shape[1]
    slot_cap = max(4, 2 * tok_rows * top_count // experts)
    order = lax.rem(me + jnp.array([0, 3, 1, 2], jnp.int32), tp_size)

    def exchange(value):
        return [value, shift(value, 1), shift(value, -1), shift(value, 2)]

    def in_order(value):
        stack = jnp.zeros((tp_size,) + value.shape, value.dtype)
        for place, piece in enumerate(exchange(value)):
            stack = lax.dynamic_update_slice_in_dim(stack, piece[None], order[place], 0)
        return stack

    expert_ids = jnp.arange(experts, dtype=jnp.int32)
    named = jnp.any(routes[:, :, None] == expert_ids[None, None, :], axis=1)
    token_ids = jnp.arange(tok_rows, dtype=jnp.int32)
    earlier = (token_ids[None, :] < token_ids[:, None]).astype(BF16)
    my_places = jnp.dot(earlier, named.astype(BF16), preferred_element_type=F32)
    my_places = jnp.where(named, my_places, -1.0).astype(BF16)
    groups = width // tok_rows
    extra = my_places.T.reshape(groups, -1, tok_rows).transpose(1, 0, 2).reshape(-1, width)

    chunk_a, chunk_b = run_columns(
        order, exchange(audio_feats), w_audio, b_audio.reshape(tp_size, width), extra
    )
    parts_a = exchange(chunk_a)
    chunk_b, _ = lax.optimization_barrier((chunk_b, parts_a[1]))
    parts_b = exchange(chunk_b)

    cos, sin = rope_tables(seq_len, head_dim)
    seg = (segments.reshape(seq_len, 1), segments)
    by_device = (tp_size, width)
    half = seq_len // 2

    def layer(first, parts, past):
        *pieces, keys, values = run_layer(
            order, parts, half, past, first, attn_gain[None], w_q, w_k, w_v, w_o,
            q_gain[None], k_gain[None], cos, sin, seg,
        )
        return pieces, (keys, values)

    def summands(pieces):
        to_right, to_left, to_opposite, mine = pieces
        return [shift(to_right, 1), shift(to_left, -1), shift(to_opposite, 2), mine]

    pieces_a, past = layer(0, parts_a, ())
    pieces_b, _ = layer(half, parts_b, past)
    tables, pieces_b = lax.optimization_barrier((parts_a, pieces_b))
    count = 2
    met = run_chosen(order, tables, tok_rows, experts, slot_cap, count)
    terms = (summands(pieces_a), summands(pieces_b))
    blocks = jnp.concatenate(
        [
            (sum(piece.astype(F32) for piece in term) + chunk.astype(F32)).astype(BF16)
            for chunk, term in zip((chunk_a[:half], chunk_b), terms)
        ],
        axis=0,
    )

    def travel(rows):
        return lax.all_to_all(rows, ("exp", "tp"), 0, 0, tiled=True)

    results = []
    for chosen in met:
        rows = jnp.dot(chosen.reshape(-1, seq_len), blocks, preferred_element_type=F32)
        arrived = travel(rows.astype(BF16).reshape(experts, -1, width))
        results.append(
            run_experts(
                arrived.reshape(-1, tp_size, arrived.shape[1], width),
                moe_gain.reshape(by_device), w_gate_up[0], w_down[0],
            ).reshape(experts, -1, feat_dim)
        )

    blocks, _ = lax.optimization_barrier((blocks, results[0]))
    blocks = blocks.reshape(tp_size, tok_rows, width)

    def block_of(place):
        return lax.dynamic_index_in_dim(blocks, order[place], 0, keepdims=False)

    own = [block_of(0), shift(block_of(2), 1), shift(block_of(1), -1), shift(block_of(3), 2)]
    results[1], own = lax.optimization_barrier((results[1], own))
    hidden_res = run_join(order, own)
    hidden_res = hidden_res.astype(F32)
    returned = [travel(rows).reshape(-1, feat_dim) for rows in results]
    squares = jnp.mean(hidden_res * hidden_res, axis=-1, keepdims=True)
    normed = (hidden_res * lax.rsqrt(squares + EPSILON) * moe_gain).astype(BF16)

    logits = jnp.dot(normed, w_router, preferred_element_type=F32)
    peak = jnp.max(jnp.where(named, logits, -jnp.inf), axis=1, keepdims=True)
    expo = jnp.where(named, jnp.exp(jnp.minimum(logits - peak, 0.0)), 0.0)
    gates = (expo / jnp.sum(expo, axis=1, keepdims=True)).astype(BF16)
    part_cap = slot_cap // count
    slot_of = jnp.arange(experts * part_cap, dtype=jnp.int32)
    spread = (expert_ids[:, None] == (slot_of // part_cap)[None, :]).astype(BF16)
    wide_gates = jnp.dot(gates, spread, preferred_element_type=F32)
    wide_places = jnp.dot(my_places, spread, preferred_element_type=F32)
    total = hidden_res
    for part in range(count):
        slot = (slot_of % part_cap + part * part_cap).astype(F32)
        combine = jnp.where(wide_places == slot[None, :], wide_gates, 0.0).astype(BF16)
        total = total + jnp.dot(combine, returned[part], preferred_element_type=F32)
    return total.astype(BF16)


def solution(mesh):
    in_specs = (
        P(("exp", "tp"), None),
        P(None, "tp"),
        P(),
        P("exp", None),
        P(None, "tp"),
        P(None, "tp"),
        P(None, "tp"),
        P("tp", None),
        P(),
        P(),
        P(),
        P(),
        P(),
        P(("exp", "tp"), None),
        P(("exp", "tp"), None, None),
        P(("exp", "tp"), None, None),
    )
    out_specs = P(("exp", "tp"), None)
    return jax.shard_map(
        on_device, mesh=mesh, in_specs=in_specs, out_specs=out_specs, check_vma=False
    )
```

```python
import math

import jax
import jax.numpy as jnp
from jax import lax
from jax.experimental import pallas as pl
from jax.experimental.pallas import tpu as pltpu
from jax.sharding import PartitionSpec as P

EPSILON = 1e-06
ROPE_BASE = 1000000.0
F32 = jnp.float32
BF16 = jnp.bfloat16
VMEM_BYTES = 32 * 1024 * 1024
EXPERT_VMEM_BYTES = 56 * 1024 * 1024


def whole(count):
    return [pl.BlockSpec(memory_space=pltpu.VMEM)] * count


def far(count):
    return [pl.BlockSpec(memory_space=pltpu.HBM)] * count


def in_far(values):
    return [pltpu.with_memory_space_constraint(value, pltpu.HBM) for value in values]


def shift(value, by):
    size = lax.axis_size("tp")
    return lax.ppermute(value, "tp", [(i, (i + by) % size) for i in range(size)])


def rope_tables(seq_len, head_dim):
    half_dim = head_dim // 2
    inv_freq = ROPE_BASE ** (-(jnp.arange(half_dim, dtype=F32) * 2.0) / head_dim)
    angles = jnp.arange(seq_len, dtype=F32)[:, None] * inv_freq[None, :]
    cos, sin = jnp.cos(angles), jnp.sin(angles)
    return jnp.concatenate([cos, cos], axis=1), jnp.concatenate([-sin, sin], axis=1)


def columns_kernel(order, own, left, right, opposite, far_weight, bias, extra, first, second, near, weight, sems):
    sources = (own, left, right, opposite)
    rows = own.shape[0]
    some = second.shape[0] // rows
    copies = [
        pltpu.make_async_copy(source, near.at[place], sems.at[place])
        for place, source in enumerate(sources)
    ]
    last = pltpu.make_async_copy(far_weight, weight, sems.at[4])
    last.start()
    for copy in copies:
        copy.start()
    first[pl.ds(some * rows, extra.shape[0]), :] = extra[...]
    part = bias[pl.ds(order[0], 1), :]
    last.wait()
    for place, copy in enumerate(copies):
        copy.wait()
        product = jnp.dot(near[place], weight[...], preferred_element_type=F32)
        product = (product + part).astype(BF16)
        at = order[place]
        for number in range(2 * some):
            out = (first, second)[number // some]

            @pl.when(at == number)
            def _():
                out[pl.ds(number % some * rows, rows), :] = product


def run_columns(order, pieces, weight, bias, extra):
    rows, depth = pieces[0].shape
    width = weight.shape[1]
    half = jax.ShapeDtypeStruct((2 * rows, width), BF16)
    longer = jax.ShapeDtypeStruct((2 * rows + extra.shape[0], width), BF16)
    return pl.pallas_call(
        columns_kernel,
        in_specs=[pl.BlockSpec(memory_space=pltpu.SMEM)] + far(5) + whole(2),
        out_specs=whole(2),
        out_shape=(longer, half),
        scratch_shapes=[
            pltpu.VMEM((4, rows, depth), BF16),
            pltpu.VMEM(weight.shape, BF16),
            pltpu.SemaphoreType.DMA((5,)),
        ],
        compiler_params=pltpu.CompilerParams(vmem_limit_bytes=VMEM_BYTES),
        cost_estimate=pl.CostEstimate(
            flops=8 * rows * weight.size, transcendentals=0,
            bytes_accessed=2 * weight.size + 8 * pieces[0].size,
        ),
        name="columns",
    )(order, *in_far(pieces[:1]), *pieces[1:], *in_far([weight]), bias, extra)


def chosen_kernel(order, own, left, right, opposite, *outs):
    experts, pairs, rows, columns = outs[0].shape
    cap = rows // 2
    tokens = columns // (2 * pairs)
    some = own.shape[0]
    row = lax.broadcasted_iota(jnp.int32, (some, rows, tokens), 1)
    for place, piece in enumerate((own, left, right, opposite)):
        at = order[place]
        pair = at // 2
        here_columns = pl.ds(pl.multiple_of(at * tokens, tokens), tokens)
        slots = [
            jnp.where(row // cap == at % 2, row % cap + which * cap, -2).astype(F32)
            for which in range(len(outs))
        ]

        def body(part, carry):
            places = piece[:, pl.ds(pl.multiple_of(part * tokens, tokens), tokens)].astype(F32)
            places = jnp.broadcast_to(places[:, None, :], row.shape)
            here = pl.ds(part * some, some)
            for slot, out in zip(slots, outs):
                met = (places == slot).astype(F32).astype(BF16)
                out[here, pair, :, here_columns] = met
                out[here, pairs - 1 - pair, :, here_columns] = jnp.zeros_like(met)
            return carry

        lax.fori_loop(0, experts // some, body, 0)


def run_chosen(order, parts, tokens, experts, cap, count):
    rows, width = parts[0].shape
    some = experts * tokens // width
    table = pl.BlockSpec((some, width), lambda i: (rows // some - 1, 0))
    shape = (experts, 2, 2 * cap // count, 4 * tokens)
    result = pl.BlockSpec(shape, lambda i: (0, 0, 0, 0))
    return pl.pallas_call(
        chosen_kernel,
        grid=(1,),
        in_specs=[pl.BlockSpec(memory_space=pltpu.SMEM)] + [table] * 4,
        out_specs=[result] * count,
        out_shape=(jax.ShapeDtypeStruct(shape, BF16),) * count,
        compiler_params=pltpu.CompilerParams(vmem_limit_bytes=VMEM_BYTES),
        name="chosen",
    )(order, *parts)


def layer_kernel(*refs, first):
    order, sources, refs = refs[0], refs[1:5], refs[5:]
    if first:
        past_keys, past_values = refs[:2]
        refs = refs[2:]
    weights, refs = refs[:4], refs[4:]
    (gain, q_gain, k_gain, cos, sin, seg_col, seg_row,
     to_right, to_left, to_opposite, to_own, keys_out, values_out,
     normed, queries, keys, values, context, near, w_k, w_v, w_q, w_o, sems) = refs
    count, width = to_own.shape
    feat_dim = w_q.shape[0]
    head_dim = w_k.shape[1]
    heads = queries.shape[0]
    block = 128
    factor = float(head_dim) ** -0.5 * math.log2(math.e)

    copies = [
        pltpu.make_async_copy(source.at[pl.ds(0, count), :], near.at[place], sems.at[place])
        for place, source in enumerate(sources)
    ] + [
        pltpu.make_async_copy(source, target, sems.at[4 + place])
        for place, (source, target) in enumerate(zip(weights, (w_k, w_v, w_q, w_o)))
    ]
    for copy in copies:
        copy.start()
    for copy in copies[:4]:
        copy.wait()

    pieces = [near[place].astype(F32) for place in range(4)]
    squares = sum(jnp.sum(piece * piece, axis=1, keepdims=True) for piece in pieces)
    scale = lax.rsqrt(squares / feat_dim + EPSILON)
    for place, piece in enumerate(pieces):
        at = order[place]
        columns = pl.ds(pl.multiple_of(at * width, width), width)
        normed[:, columns] = (piece * scale * gain[:, columns]).astype(BF16)

    here = pl.ds(first, count)
    turn_cos, turn_sin = cos[here, :], sin[here, :]

    def head_of(raw, head_gain):
        squares = jnp.mean(raw * raw, axis=1, keepdims=True)
        raw = raw * lax.rsqrt(squares + EPSILON) * head_gain[...]
        return (raw * turn_cos + pltpu.roll(raw, head_dim // 2, 1) * turn_sin).astype(BF16)

    if first:
        keys[:first, :] = past_keys[...]
        values[:first, :] = past_values[...]
    copies[4].wait()
    new_keys = head_of(jnp.dot(normed[...], w_k[...], preferred_element_type=F32), k_gain)
    copies[5].wait()
    new_values = jnp.dot(normed[...], w_v[...], preferred_element_type=F32).astype(BF16)
    keys[here, :] = new_keys
    values[here, :] = new_values
    keys_out[...] = new_keys
    values_out[...] = new_values
    copies[6].wait()
    for pair in range(heads // 2):
        raw = jnp.dot(
            normed[...], w_q[:, pl.ds(pair * 2 * head_dim, 2 * head_dim)],
            preferred_element_type=F32,
        )
        for one in range(2):
            queries[2 * pair + one] = head_of(raw[:, one * head_dim : (one + 1) * head_dim], q_gain)

    for start in range(0, count, block):
        span = first + start + block
        row_at = first + start + lax.broadcasted_iota(jnp.int32, (block, span), 0)
        col_at = lax.broadcasted_iota(jnp.int32, (block, span), 1)
        same = seg_col[pl.ds(first + start, block), :] == seg_row[:, :span]
        allowed = same & (col_at <= row_at)
        for head in range(heads):
            scores = lax.dot_general(
                queries[head, pl.ds(start, block), :], keys[:span, :], (((1,), (1,)), ((), ())),
                preferred_element_type=F32,
            )
            scores = jnp.where(allowed, scores, -1e30)
            expo = jnp.exp2((scores - jnp.max(scores, axis=1, keepdims=True)) * factor)
            total = jnp.sum(expo, axis=1, keepdims=True)
            mixed = jnp.dot(expo.astype(BF16), values[:span, :], preferred_element_type=F32)
            context[pl.ds(start, block), pl.ds(head * head_dim, head_dim)] = (
                mixed / total
            ).astype(BF16)

    copies[7].wait()
    for place, out in ((2, to_right), (1, to_left), (3, to_opposite), (0, to_own)):
        columns = pl.ds(pl.multiple_of(order[place] * width, width), width)
        out[...] = jnp.dot(context[...], w_o[:, columns], preferred_element_type=F32).astype(BF16)


def run_layer(
    order, parts, count, past, first, gain, w_q, w_k, w_v, w_o, q_gain, k_gain, cos, sin, seg
):
    width = parts[0].shape[1]
    feat_dim = w_q.shape[0]
    head_dim = w_k.shape[1]
    heads = w_q.shape[1] // head_dim
    span = first + count
    piece = jax.ShapeDtypeStruct((count, width), BF16)
    kv = jax.ShapeDtypeStruct((count, head_dim), BF16)
    weights = (w_k, w_v, w_q, w_o)
    operands = [*parts, *past, *in_far(weights), gain, q_gain, k_gain, cos, sin, *seg]

    def kernel(*refs):
        layer_kernel(*refs, first=first)

    return pl.pallas_call(
        kernel,
        in_specs=[pl.BlockSpec(memory_space=pltpu.SMEM)]
        + far(len(parts)) + whole(len(past)) + far(len(weights))
        + whole(len(operands) - len(parts) - len(past) - len(weights)),
        out_specs=whole(6),
        out_shape=(piece,) * 4 + (kv,) * 2,
        scratch_shapes=[
            pltpu.VMEM((count, feat_dim), BF16),
            pltpu.VMEM((heads, count, head_dim), BF16),
            pltpu.VMEM((span, head_dim), BF16),
            pltpu.VMEM((span, head_dim), BF16),
            pltpu.VMEM((count, heads * head_dim), BF16),
            pltpu.VMEM((len(parts), count, width), BF16),
        ]
        + [pltpu.VMEM(weight.shape, BF16) for weight in weights]
        + [pltpu.SemaphoreType.DMA((len(parts) + len(weights),))],
        compiler_params=pltpu.CompilerParams(vmem_limit_bytes=VMEM_BYTES),
        cost_estimate=pl.CostEstimate(
            flops=4 * count * feat_dim * (heads + 1) * head_dim
            + 4 * count * span * heads * head_dim,
            transcendentals=count * span * heads,
            bytes_accessed=4 * feat_dim * (heads + 1) * head_dim + 16 * count * width,
        ),
        name="layer",
    )(order, *operands)


def expert_kernel(rows, gain, w_gate_up, w_down, out, normed):
    groups, parts, slots, width = rows.shape
    count = groups * slots
    feat_dim = parts * width
    inner = w_down.shape[0]
    pieces = [rows[:, part].reshape(count, width).astype(F32) for part in range(parts)]
    squares = sum(jnp.sum(piece * piece, axis=1, keepdims=True) for piece in pieces)
    scale = lax.rsqrt(squares / feat_dim + EPSILON)
    for part, piece in enumerate(pieces):
        normed[:, pl.ds(part * width, width)] = (
            piece * scale * gain[pl.ds(part, 1), :]
        ).astype(BF16)
    both = jnp.dot(normed[...], w_gate_up[...], preferred_element_type=F32)
    gate, up = both[:, :inner], both[:, inner:]
    hidden = (gate * jax.nn.sigmoid(gate) * up).astype(BF16)
    result = jnp.dot(hidden, w_down[...], preferred_element_type=F32)
    out[...] = result.astype(BF16)


def run_experts(arrived, gain, w_gate_up, w_down):
    sources, parts, slots, width = arrived.shape
    feat_dim, double = w_gate_up.shape
    groups = 8

    def fixed(shape):
        return pl.BlockSpec(shape, lambda i: (0, 0), pipeline_mode=pl.Buffered(1))

    return pl.pallas_call(
        expert_kernel,
        grid=(sources // groups,),
        in_specs=[
            pl.BlockSpec((groups, parts, slots, width), lambda i: (i, 0, 0, 0)),
            fixed(gain.shape), fixed(w_gate_up.shape), fixed(w_down.shape),
        ],
        out_specs=pl.BlockSpec((groups * slots, feat_dim), lambda i: (i, 0)),
        out_shape=pltpu.HBM((sources * slots, feat_dim), BF16),
        scratch_shapes=[pltpu.VMEM((groups * slots, feat_dim), BF16)],
        compiler_params=pltpu.CompilerParams(vmem_limit_bytes=EXPERT_VMEM_BYTES),
        cost_estimate=pl.CostEstimate(
            flops=3 * sources * slots * feat_dim * double,
            transcendentals=sources * slots * double // 2,
            bytes_accessed=4 * sources * slots * feat_dim + 3 * feat_dim * double,
        ),
        name="experts",
    )(*in_far([arrived]), gain, *in_far([w_gate_up, w_down]))


def join_kernel(order, own, left, right, opposite, out):
    width = own.shape[1]
    for place, piece in enumerate((own, left, right, opposite)):
        out[:, pl.ds(pl.multiple_of(order[place] * width, width), width)] = piece[...]


def run_join(order, pieces):
    count, width = pieces[0].shape
    return pl.pallas_call(
        join_kernel,
        in_specs=[pl.BlockSpec(memory_space=pltpu.SMEM)] + whole(4),
        out_specs=whole(1)[0],
        out_shape=jax.ShapeDtypeStruct((count, 4 * width), BF16),
        name="join",
    )(order, *pieces)


def on_device(
    audio_feats, w_audio, b_audio, segments, w_q, w_k, w_v, w_o, attn_gain, q_gain, k_gain,
    moe_gain, w_router, routes, w_gate_up, w_down,
):
    me = lax.axis_index("tp")
    tp_size = lax.axis_size("tp")
    tok_rows = audio_feats.shape[0]
    feat_dim = b_audio.shape[0]
    seq_len = segments.shape[1]
    head_dim = q_gain.shape[0]
    experts = w_router.shape[1]
    top_count = routes.shape[1]
    width = w_audio.shape[1]
    slot_cap = max(4, 2 * tok_rows * top_count // experts)
    order = lax.rem(me + jnp.array([0, 3, 1, 2], jnp.int32), tp_size)

    def exchange(value):
        return [value, shift(value, 1), shift(value, -1), shift(value, 2)]

    def in_order(value):
        stack = jnp.zeros((tp_size,) + value.shape, value.dtype)
        for place, piece in enumerate(exchange(value)):
            stack = lax.dynamic_update_slice_in_dim(stack, piece[None], order[place], 0)
        return stack

    expert_ids = jnp.arange(experts, dtype=jnp.int32)
    named = jnp.any(routes[:, :, None] == expert_ids[None, None, :], axis=1)
    token_ids = jnp.arange(tok_rows, dtype=jnp.int32)
    earlier = (token_ids[None, :] < token_ids[:, None]).astype(BF16)
    my_places = jnp.dot(earlier, named.astype(BF16), preferred_element_type=F32)
    my_places = jnp.where(named, my_places, -1.0).astype(BF16)
    groups = width // tok_rows
    extra = my_places.T.reshape(groups, -1, tok_rows).transpose(1, 0, 2).reshape(-1, width)

    chunk_a, chunk_b = run_columns(
        order, exchange(audio_feats), w_audio, b_audio.reshape(tp_size, width), extra
    )
    parts_a = exchange(chunk_a)
    chunk_b, _ = lax.optimization_barrier((chunk_b, parts_a[1]))
    parts_b = exchange(chunk_b)

    cos, sin = rope_tables(seq_len, head_dim)
    seg = (segments.reshape(seq_len, 1), segments)
    by_device = (tp_size, width)
    half = seq_len // 2

    def layer(first, parts, past):
        *pieces, keys, values = run_layer(
            order, parts, half, past, first, attn_gain[None], w_q, w_k, w_v, w_o,
            q_gain[None], k_gain[None], cos, sin, seg,
        )
        return pieces, (keys, values)

    def summands(pieces):
        to_right, to_left, to_opposite, mine = pieces
        return [shift(to_right, 1), shift(to_left, -1), shift(to_opposite, 2), mine]

    pieces_a, past = layer(0, parts_a, ())
    pieces_b, _ = layer(half, parts_b, past)
    tables, pieces_b = lax.optimization_barrier((parts_a, pieces_b))
    count = 2
    met = run_chosen(order, tables, tok_rows, experts, slot_cap, count)
    terms = (summands(pieces_a), summands(pieces_b))
    blocks = jnp.concatenate(
        [
            (sum(piece.astype(F32) for piece in term) + chunk.astype(F32)).astype(BF16)
            for chunk, term in zip((chunk_a[:half], chunk_b), terms)
        ],
        axis=0,
    )

    def travel(rows):
        return lax.all_to_all(rows, ("exp", "tp"), 0, 0, tiled=True)

    results = []
    for chosen in met:
        rows = jnp.dot(chosen.reshape(-1, seq_len), blocks, preferred_element_type=F32)
        arrived = travel(rows.astype(BF16).reshape(experts, -1, width))
        results.append(
            run_experts(
                arrived.reshape(-1, tp_size, arrived.shape[1], width),
                moe_gain.reshape(by_device), w_gate_up[0], w_down[0],
            ).reshape(experts, -1, feat_dim)
        )

    blocks, _ = lax.optimization_barrier((blocks, results[0]))
    blocks = blocks.reshape(tp_size, tok_rows, width)

    def block_of(place):
        return lax.dynamic_index_in_dim(blocks, order[place], 0, keepdims=False)

    own = [block_of(0), shift(block_of(2), 1), shift(block_of(1), -1), shift(block_of(3), 2)]
    results[1], own = lax.optimization_barrier((results[1], own))
    hidden_res = run_join(order, own)
    hidden_res = hidden_res.astype(F32)
    returned = [travel(rows).reshape(-1, feat_dim) for rows in results]
    squares = jnp.mean(hidden_res * hidden_res, axis=-1, keepdims=True)
    normed = (hidden_res * lax.rsqrt(squares + EPSILON) * moe_gain).astype(BF16)

    logits = jnp.dot(normed, w_router, preferred_element_type=F32)
    peak = jnp.max(jnp.where(named, logits, -jnp.inf), axis=1, keepdims=True)
    expo = jnp.where(named, jnp.exp(jnp.minimum(logits - peak, 0.0)), 0.0)
    gates = (expo / jnp.sum(expo, axis=1, keepdims=True)).astype(BF16)
    part_cap = slot_cap // count
    slot_of = jnp.arange(experts * part_cap, dtype=jnp.int32)
    spread = (expert_ids[:, None] == (slot_of // part_cap)[None, :]).astype(BF16)
    wide_gates = jnp.dot(gates, spread, preferred_element_type=F32)
    wide_places = jnp.dot(my_places, spread, preferred_element_type=F32)
    total = hidden_res
    for part in range(count):
        slot = (slot_of % part_cap + part * part_cap).astype(F32)
        combine = jnp.where(wide_places == slot[None, :], wide_gates, 0.0).astype(BF16)
        total = total + jnp.dot(combine, returned[part], preferred_element_type=F32)
    return total.astype(BF16)


def solution(mesh):
    in_specs = (
        P(("exp", "tp"), None),
        P(None, "tp"),
        P(),
        P("exp", None),
        P(None, "tp"),
        P(None, "tp"),
        P(None, "tp"),
        P("tp", None),
        P(),
        P(),
        P(),
        P(),
        P(),
        P(("exp", "tp"), None),
        P(("exp", "tp"), None, None),
        P(("exp", "tp"), None, None),
    )
    out_specs = P(("exp", "tp"), None)
    return jax.shard_map(
        on_device, mesh=mesh, in_specs=in_specs, out_specs=out_specs, check_vma=False
    )
```

```python
import math

import jax
import jax.numpy as jnp
from jax import lax
from jax.experimental import pallas as pl
from jax.experimental.pallas import tpu as pltpu
from jax.sharding import PartitionSpec as P

EPSILON = 1e-06
ROPE_BASE = 1000000.0
F32 = jnp.float32
BF16 = jnp.bfloat16
VMEM_BYTES = 32 * 1024 * 1024
EXPERT_VMEM_BYTES = 56 * 1024 * 1024


def whole(count):
    return [pl.BlockSpec(memory_space=pltpu.VMEM)] * count


def far(count):
    return [pl.BlockSpec(memory_space=pltpu.HBM)] * count


def in_far(values):
    return [pltpu.with_memory_space_constraint(value, pltpu.HBM) for value in values]


def shift(value, by):
    size = lax.axis_size("tp")
    return lax.ppermute(value, "tp", [(i, (i + by) % size) for i in range(size)])


def rope_tables(seq_len, head_dim):
    half_dim = head_dim // 2
    inv_freq = ROPE_BASE ** (-(jnp.arange(half_dim, dtype=F32) * 2.0) / head_dim)
    angles = jnp.arange(seq_len, dtype=F32)[:, None] * inv_freq[None, :]
    cos, sin = jnp.cos(angles), jnp.sin(angles)
    return jnp.concatenate([cos, cos], axis=1), jnp.concatenate([-sin, sin], axis=1)


def columns_kernel(order, own, left, right, opposite, far_weight, bias, extra, first, second, near, weight, sems):
    sources = (own, left, right, opposite)
    rows = own.shape[0]
    some = second.shape[0] // rows
    copies = [
        pltpu.make_async_copy(source, near.at[place], sems.at[place])
        for place, source in enumerate(sources)
    ]
    last = pltpu.make_async_copy(far_weight, weight, sems.at[4])
    last.start()
    for copy in copies:
        copy.start()
    first[pl.ds(some * rows, extra.shape[0]), :] = extra[...]
    part = bias[pl.ds(order[0], 1), :]
    last.wait()
    for copy in copies:
        copy.wait()
    frames = near[...].reshape(-1, near.shape[-1])
    columns = jnp.dot(frames, weight[...], preferred_element_type=F32)
    columns = (columns + part).astype(BF16)
    for place in range(len(copies)):
        product = columns[place * rows : (place + 1) * rows]
        at = order[place]
        for number in range(2 * some):
            out = (first, second)[number // some]

            @pl.when(at == number)
            def _():
                out[pl.ds(number % some * rows, rows), :] = product


def run_columns(order, pieces, weight, bias, extra):
    rows, depth = pieces[0].shape
    width = weight.shape[1]
    half = jax.ShapeDtypeStruct((2 * rows, width), BF16)
    longer = jax.ShapeDtypeStruct((2 * rows + extra.shape[0], width), BF16)
    return pl.pallas_call(
        columns_kernel,
        in_specs=[pl.BlockSpec(memory_space=pltpu.SMEM)] + far(5) + whole(2),
        out_specs=whole(2),
        out_shape=(longer, half),
        scratch_shapes=[
            pltpu.VMEM((4, rows, depth), BF16),
            pltpu.VMEM(weight.shape, BF16),
            pltpu.SemaphoreType.DMA((5,)),
        ],
        compiler_params=pltpu.CompilerParams(vmem_limit_bytes=VMEM_BYTES),
        cost_estimate=pl.CostEstimate(
            flops=8 * rows * weight.size, transcendentals=0,
            bytes_accessed=2 * weight.size + 8 * pieces[0].size,
        ),
        name="columns",
    )(order, *in_far(pieces[:1]), *pieces[1:], *in_far([weight]), bias, extra)


def chosen_kernel(order, own, left, right, opposite, *outs):
    experts, pairs, rows, columns = outs[0].shape
    cap = rows // 2
    tokens = columns // (2 * pairs)
    some = own.shape[0]
    row = lax.broadcasted_iota(jnp.int32, (some, rows, tokens), 1)
    for place, piece in enumerate((own, left, right, opposite)):
        at = order[place]
        pair = at // 2
        here_columns = pl.ds(pl.multiple_of(at * tokens, tokens), tokens)
        slots = [
            jnp.where(row // cap == at % 2, row % cap + which * cap, -2).astype(F32)
            for which in range(len(outs))
        ]

        def body(part, carry):
            places = piece[:, pl.ds(pl.multiple_of(part * tokens, tokens), tokens)].astype(F32)
            places = jnp.broadcast_to(places[:, None, :], row.shape)
            here = pl.ds(part * some, some)
            for slot, out in zip(slots, outs):
                met = (places == slot).astype(F32).astype(BF16)
                out[here, pair, :, here_columns] = met
                out[here, pairs - 1 - pair, :, here_columns] = jnp.zeros_like(met)
            return carry

        lax.fori_loop(0, experts // some, body, 0)


def run_chosen(order, parts, tokens, experts, cap, count):
    rows, width = parts[0].shape
    some = experts * tokens // width
    table = pl.BlockSpec((some, width), lambda i: (rows // some - 1, 0))
    shape = (experts, 2, 2 * cap // count, 4 * tokens)
    result = pl.BlockSpec(shape, lambda i: (0, 0, 0, 0))
    return pl.pallas_call(
        chosen_kernel,
        grid=(1,),
        in_specs=[pl.BlockSpec(memory_space=pltpu.SMEM)] + [table] * 4,
        out_specs=[result] * count,
        out_shape=(jax.ShapeDtypeStruct(shape, BF16),) * count,
        compiler_params=pltpu.CompilerParams(vmem_limit_bytes=VMEM_BYTES),
        name="chosen",
    )(order, *parts)


def layer_kernel(*refs, first):
    order, sources, refs = refs[0], refs[1:5], refs[5:]
    if first:
        past_keys, past_values = refs[:2]
        refs = refs[2:]
    weights, refs = refs[:4], refs[4:]
    (gain, q_gain, k_gain, cos, sin, seg_col, seg_row,
     to_right, to_left, to_opposite, to_own, keys_out, values_out,
     normed, queries, keys, values, context, near, w_k, w_v, w_q, w_o, sems) = refs
    count, width = to_own.shape
    feat_dim = w_q.shape[0]
    head_dim = w_k.shape[1]
    heads = queries.shape[0]
    block = 128
    factor = float(head_dim) ** -0.5 * math.log2(math.e)

    copies = [
        pltpu.make_async_copy(source.at[pl.ds(0, count), :], near.at[place], sems.at[place])
        for place, source in enumerate(sources)
    ]
    split = {}
    for place, (source, target) in enumerate(zip(weights, (w_k, w_v, w_q, w_o))):
        count_of = 1 if place < 2 else 4
        depth = target.shape[0] // count_of
        split[place] = [
            pltpu.make_async_copy(
                source.at[pl.ds(part * depth, depth), :], target.at[pl.ds(part * depth, depth), :],
                sems.at[4 + 4 * place + part],
            )
            for part in range(count_of)
        ]
    for copy in copies + split[0] + split[1] + split[2] + split[3]:
        copy.start()
    for copy in copies:
        copy.wait()

    pieces = [near[place].astype(F32) for place in range(4)]
    squares = sum(jnp.sum(piece * piece, axis=1, keepdims=True) for piece in pieces)
    scale = lax.rsqrt(squares / feat_dim + EPSILON)
    for place, piece in enumerate(pieces):
        at = order[place]
        columns = pl.ds(pl.multiple_of(at * width, width), width)
        normed[:, columns] = (piece * scale * gain[:, columns]).astype(BF16)

    here = pl.ds(first, count)
    turn_cos, turn_sin = cos[here, :], sin[here, :]

    def head_of(raw, head_gain):
        squares = jnp.mean(raw * raw, axis=1, keepdims=True)
        raw = raw * lax.rsqrt(squares + EPSILON) * head_gain[...]
        return (raw * turn_cos + pltpu.roll(raw, head_dim // 2, 1) * turn_sin).astype(BF16)

    if first:
        keys[:first, :] = past_keys[...]
        values[:first, :] = past_values[...]
    for copy in split[0]:
        copy.wait()
    new_keys = head_of(jnp.dot(normed[...], w_k[...], preferred_element_type=F32), k_gain)
    for copy in split[1]:
        copy.wait()
    new_values = jnp.dot(normed[...], w_v[...], preferred_element_type=F32).astype(BF16)
    keys[here, :] = new_keys
    values[here, :] = new_values
    keys_out[...] = new_keys
    values_out[...] = new_values
    for copy in split[2]:
        copy.wait()
    for pair in range(heads // 2):
        raw = jnp.dot(
            normed[...], w_q[:, pl.ds(pair * 2 * head_dim, 2 * head_dim)],
            preferred_element_type=F32,
        )
        for one in range(2):
            queries[2 * pair + one] = head_of(raw[:, one * head_dim : (one + 1) * head_dim], q_gain)

    for start in range(0, count, block):
        span = first + start + block
        row_at = first + start + lax.broadcasted_iota(jnp.int32, (block, span), 0)
        col_at = lax.broadcasted_iota(jnp.int32, (block, span), 1)
        same = seg_col[pl.ds(first + start, block), :] == seg_row[:, :span]
        allowed = same & (col_at <= row_at)
        for head in range(heads):
            scores = lax.dot_general(
                queries[head, pl.ds(start, block), :], keys[:span, :], (((1,), (1,)), ((), ())),
                preferred_element_type=F32,
            )
            scores = jnp.where(allowed, scores, -1e30)
            expo = jnp.exp2((scores - jnp.max(scores, axis=1, keepdims=True)) * factor)
            total = jnp.sum(expo, axis=1, keepdims=True)
            mixed = jnp.dot(expo.astype(BF16), values[:span, :], preferred_element_type=F32)
            context[pl.ds(start, block), pl.ds(head * head_dim, head_dim)] = (
                mixed / total
            ).astype(BF16)

    for copy in split[3]:
        copy.wait()
    for place, out in ((2, to_right), (1, to_left), (3, to_opposite), (0, to_own)):
        columns = pl.ds(pl.multiple_of(order[place] * width, width), width)
        out[...] = jnp.dot(context[...], w_o[:, columns], preferred_element_type=F32).astype(BF16)


def run_layer(
    order, parts, count, past, first, gain, w_q, w_k, w_v, w_o, q_gain, k_gain, cos, sin, seg
):
    width = parts[0].shape[1]
    feat_dim = w_q.shape[0]
    head_dim = w_k.shape[1]
    heads = w_q.shape[1] // head_dim
    span = first + count
    piece = jax.ShapeDtypeStruct((count, width), BF16)
    kv = jax.ShapeDtypeStruct((count, head_dim), BF16)
    weights = (w_k, w_v, w_q, w_o)
    operands = [*parts, *past, *in_far(weights), gain, q_gain, k_gain, cos, sin, *seg]

    def kernel(*refs):
        layer_kernel(*refs, first=first)

    return pl.pallas_call(
        kernel,
        in_specs=[pl.BlockSpec(memory_space=pltpu.SMEM)]
        + far(len(parts)) + whole(len(past)) + far(len(weights))
        + whole(len(operands) - len(parts) - len(past) - len(weights)),
        out_specs=whole(6),
        out_shape=(piece,) * 4 + (kv,) * 2,
        scratch_shapes=[
            pltpu.VMEM((count, feat_dim), BF16),
            pltpu.VMEM((heads, count, head_dim), BF16),
            pltpu.VMEM((span, head_dim), BF16),
            pltpu.VMEM((span, head_dim), BF16),
            pltpu.VMEM((count, heads * head_dim), BF16),
            pltpu.VMEM((len(parts), count, width), BF16),
        ]
        + [pltpu.VMEM(weight.shape, BF16) for weight in weights]
        + [pltpu.SemaphoreType.DMA((len(parts) + 4 * len(weights),))],
        compiler_params=pltpu.CompilerParams(vmem_limit_bytes=VMEM_BYTES),
        cost_estimate=pl.CostEstimate(
            flops=4 * count * feat_dim * (heads + 1) * head_dim
            + 4 * count * span * heads * head_dim,
            transcendentals=count * span * heads,
            bytes_accessed=4 * feat_dim * (heads + 1) * head_dim + 16 * count * width,
        ),
        name="layer",
    )(order, *operands)


def expert_kernel(rows, gain, w_gate_up, w_down, out, normed):
    groups, parts, slots, width = rows.shape
    count = groups * slots
    feat_dim = parts * width
    inner = w_down.shape[0]
    pieces = [rows[:, part].reshape(count, width).astype(F32) for part in range(parts)]
    squares = sum(jnp.sum(piece * piece, axis=1, keepdims=True) for piece in pieces)
    scale = lax.rsqrt(squares / feat_dim + EPSILON)
    for part, piece in enumerate(pieces):
        normed[:, pl.ds(part * width, width)] = (
            piece * scale * gain[pl.ds(part, 1), :]
        ).astype(BF16)
    both = jnp.dot(normed[...], w_gate_up[...], preferred_element_type=F32)
    gate, up = both[:, :inner], both[:, inner:]
    hidden = (gate * jax.nn.sigmoid(gate) * up).astype(BF16)
    result = jnp.dot(hidden, w_down[...], preferred_element_type=F32)
    out[...] = result.astype(BF16)


def run_experts(arrived, gain, w_gate_up, w_down):
    sources, parts, slots, width = arrived.shape
    feat_dim, double = w_gate_up.shape
    groups = 8

    def fixed(shape):
        return pl.BlockSpec(shape, lambda i: (0, 0), pipeline_mode=pl.Buffered(1))

    return pl.pallas_call(
        expert_kernel,
        grid=(sources // groups,),
        in_specs=[
            pl.BlockSpec((groups, parts, slots, width), lambda i: (i, 0, 0, 0)),
            fixed(gain.shape), fixed(w_gate_up.shape), fixed(w_down.shape),
        ],
        out_specs=pl.BlockSpec((groups * slots, feat_dim), lambda i: (i, 0)),
        out_shape=pltpu.HBM((sources * slots, feat_dim), BF16),
        scratch_shapes=[pltpu.VMEM((groups * slots, feat_dim), BF16)],
        compiler_params=pltpu.CompilerParams(vmem_limit_bytes=EXPERT_VMEM_BYTES),
        cost_estimate=pl.CostEstimate(
            flops=3 * sources * slots * feat_dim * double,
            transcendentals=sources * slots * double // 2,
            bytes_accessed=4 * sources * slots * feat_dim + 3 * feat_dim * double,
        ),
        name="experts",
    )(*in_far([arrived]), gain, *in_far([w_gate_up, w_down]))


def join_kernel(order, own, left, right, opposite, out):
    width = own.shape[1]
    for place, piece in enumerate((own, left, right, opposite)):
        out[:, pl.ds(pl.multiple_of(order[place] * width, width), width)] = piece[...]


def run_join(order, pieces):
    count, width = pieces[0].shape
    return pl.pallas_call(
        join_kernel,
        in_specs=[pl.BlockSpec(memory_space=pltpu.SMEM)] + whole(4),
        out_specs=whole(1)[0],
        out_shape=jax.ShapeDtypeStruct((count, 4 * width), BF16),
        name="join",
    )(order, *pieces)


def on_device(
    audio_feats, w_audio, b_audio, segments, w_q, w_k, w_v, w_o, attn_gain, q_gain, k_gain,
    moe_gain, w_router, routes, w_gate_up, w_down,
):
    me = lax.axis_index("tp")
    tp_size = lax.axis_size("tp")
    tok_rows = audio_feats.shape[0]
    feat_dim = b_audio.shape[0]
    seq_len = segments.shape[1]
    head_dim = q_gain.shape[0]
    experts = w_router.shape[1]
    top_count = routes.shape[1]
    width = w_audio.shape[1]
    slot_cap = max(4, 2 * tok_rows * top_count // experts)
    order = lax.rem(me + jnp.array([0, 3, 1, 2], jnp.int32), tp_size)

    def exchange(value):
        return [value, shift(value, 1), shift(value, -1), shift(value, 2)]

    def in_order(value):
        stack = jnp.zeros((tp_size,) + value.shape, value.dtype)
        for place, piece in enumerate(exchange(value)):
            stack = lax.dynamic_update_slice_in_dim(stack, piece[None], order[place], 0)
        return stack

    expert_ids = jnp.arange(experts, dtype=jnp.int32)
    named = jnp.any(routes[:, :, None] == expert_ids[None, None, :], axis=1)
    token_ids = jnp.arange(tok_rows, dtype=jnp.int32)
    earlier = (token_ids[None, :] < token_ids[:, None]).astype(BF16)
    my_places = jnp.dot(earlier, named.astype(BF16), preferred_element_type=F32)
    my_places = jnp.where(named, my_places, -1.0).astype(BF16)
    groups = width // tok_rows
    extra = my_places.T.reshape(groups, -1, tok_rows).transpose(1, 0, 2).reshape(-1, width)

    chunk_a, chunk_b = run_columns(
        order, exchange(audio_feats), w_audio, b_audio.reshape(tp_size, width), extra
    )
    parts_a = exchange(chunk_a)
    chunk_b, _ = lax.optimization_barrier((chunk_b, parts_a[1]))
    parts_b = exchange(chunk_b)

    cos, sin = rope_tables(seq_len, head_dim)
    seg = (segments.reshape(seq_len, 1), segments)
    by_device = (tp_size, width)
    half = seq_len // 2

    def layer(first, parts, past):
        *pieces, keys, values = run_layer(
            order, parts, half, past, first, attn_gain[None], w_q, w_k, w_v, w_o,
            q_gain[None], k_gain[None], cos, sin, seg,
        )
        return pieces, (keys, values)

    def summands(pieces):
        to_right, to_left, to_opposite, mine = pieces
        return [shift(to_right, 1), shift(to_left, -1), shift(to_opposite, 2), mine]

    pieces_a, past = layer(0, parts_a, ())
    pieces_b, _ = layer(half, parts_b, past)
    tables, pieces_b = lax.optimization_barrier((parts_a, pieces_b))
    count = 2
    met = run_chosen(order, tables, tok_rows, experts, slot_cap, count)
    terms = (summands(pieces_a), summands(pieces_b))
    blocks = jnp.concatenate(
        [
            (sum(piece.astype(F32) for piece in term) + chunk.astype(F32)).astype(BF16)
            for chunk, term in zip((chunk_a[:half], chunk_b), terms)
        ],
        axis=0,
    )

    def travel(rows):
        return lax.all_to_all(rows, ("exp", "tp"), 0, 0, tiled=True)

    results = []
    for chosen in met:
        rows = jnp.dot(chosen.reshape(-1, seq_len), blocks, preferred_element_type=F32)
        arrived = travel(rows.astype(BF16).reshape(experts, -1, width))
        results.append(
            run_experts(
                arrived.reshape(-1, tp_size, arrived.shape[1], width),
                moe_gain.reshape(by_device), w_gate_up[0], w_down[0],
            ).reshape(experts, -1, feat_dim)
        )

    blocks, _ = lax.optimization_barrier((blocks, results[0]))
    blocks = blocks.reshape(tp_size, tok_rows, width)

    def block_of(place):
        return lax.dynamic_index_in_dim(blocks, order[place], 0, keepdims=False)

    own = [block_of(0), shift(block_of(2), 1), shift(block_of(1), -1), shift(block_of(3), 2)]
    results[1], own = lax.optimization_barrier((results[1], own))
    hidden_res = run_join(order, own)
    hidden_res = hidden_res.astype(F32)
    returned = [travel(rows).reshape(-1, feat_dim) for rows in results]
    squares = jnp.mean(hidden_res * hidden_res, axis=-1, keepdims=True)
    normed = (hidden_res * lax.rsqrt(squares + EPSILON) * moe_gain).astype(BF16)

    logits = jnp.dot(normed, w_router, preferred_element_type=F32)
    peak = jnp.max(jnp.where(named, logits, -jnp.inf), axis=1, keepdims=True)
    expo = jnp.where(named, jnp.exp(jnp.minimum(logits - peak, 0.0)), 0.0)
    gates = (expo / jnp.sum(expo, axis=1, keepdims=True)).astype(BF16)
    part_cap = slot_cap // count
    slot_of = jnp.arange(experts * part_cap, dtype=jnp.int32)
    spread = (expert_ids[:, None] == (slot_of // part_cap)[None, :]).astype(BF16)
    wide_gates = jnp.dot(gates, spread, preferred_element_type=F32)
    wide_places = jnp.dot(my_places, spread, preferred_element_type=F32)
    total = hidden_res
    for part in range(count):
        slot = (slot_of % part_cap + part * part_cap).astype(F32)
        combine = jnp.where(wide_places == slot[None, :], wide_gates, 0.0).astype(BF16)
        total = total + jnp.dot(combine, returned[part], preferred_element_type=F32)
    return total.astype(BF16)


def solution(mesh):
    in_specs = (
        P(("exp", "tp"), None),
        P(None, "tp"),
        P(),
        P("exp", None),
        P(None, "tp"),
        P(None, "tp"),
        P(None, "tp"),
        P("tp", None),
        P(),
        P(),
        P(),
        P(),
        P(),
        P(("exp", "tp"), None),
        P(("exp", "tp"), None, None),
        P(("exp", "tp"), None, None),
    )
    out_specs = P(("exp", "tp"), None)
    return jax.shard_map(
        on_device, mesh=mesh, in_specs=in_specs, out_specs=out_specs, check_vma=False
    )
```
